256 devices in a mesh: tm: 32 (over y_lo, z, core), mp: 8 (over x, y_hi).
Axes of the slice: x: 4, y: 4 (y_hi: 2, y_lo: 2; y = y_hi * 2 + y_lo), z: 8, core: 2. Of those that a mesh axis runs over, the one named last changes fastest.
Arguments:
- queries: bfloat16 [4096, 6144], P('tm', 'mp'), may hold values from -13.5 to 13.5
- keys: bfloat16 [4096, 6144], P('tm', 'mp'), may hold values from -13.5 to 13.5
- values: bfloat16 [4096, 6144], P('tm', 'mp'), may hold values from -6 to 6
- window: int32 [32], P('tm'), may hold values from 0 to 4, as said below
- counts: int32 [32], P('tm'), may hold values from 32 to 128, as said below
- gain: float32 [6144], P('mp'), may hold values from 0.5 to 1.5
- w_gate: bfloat16 [6144, 16384], P('mp', 'tm'), may hold values from -0.078125 to 0.078125
- w_up: bfloat16 [6144, 16384], P('mp', 'tm'), may hold values from -0.078125 to 0.078125
- w_down: bfloat16 [16384, 6144], P('tm', 'mp'), may hold values from -0.046875 to 0.046875
Outputs:
- block_out: bfloat16 [4096, 6144], P('tm', 'mp')
The draws below stay inside these ranges and needn't reach their ends.
Inputs may be any that keep to these rules, and one draw needn't show every extreme that they name: window[c] counts the prior groups group c sees; some group has 4. Group c's valid tokens fill its first counts[c] slots; some group is full.
All inputs are finite; a program needn't handle non-finite values.
Results may differ from the reference program's by a relative error of at most 0.025.
Values may be sent and summed in bfloat16 or wider, within the bound.
A program may use at most 128 MiB of HBM per device.

```python
import jax
import jax.numpy as jnp
from jax import lax

HEADS = 48
HD = 128
D = 6144
FFW = 16384
TOK_DEV = 128
WMAX = 4
NCHUNK = 32
TOKENS = 4096
N_TM = 32
N_MP = 8


def draw_queries(key, part):
    key = jax.random.fold_in(key, 21)
    drawn = jnp.clip(jax.random.normal(key, (TOKENS, D), jnp.float32), -4.5, 4.5)
    return drawn.astype(jnp.bfloat16)


def draw_keys(key, part):
    key = jax.random.fold_in(key, 22)
    drawn = jnp.clip(jax.random.normal(key, (TOKENS, D), jnp.float32), -4.5, 4.5)
    return drawn.astype(jnp.bfloat16)


def draw_window(key, part):
    key = jax.random.fold_in(key, 31)
    first, second = jax.random.split(key)
    drawn = jax.random.randint(first, (NCHUNK,), 0, WMAX + 1)
    place = jax.random.randint(second, (), 0, NCHUNK)
    return jnp.where(jnp.arange(NCHUNK) == place, WMAX, drawn).astype(jnp.int32)


def draw_counts(key, part):
    key = jax.random.fold_in(key, 41)
    first, second = jax.random.split(key)
    drawn = jax.random.randint(first, (NCHUNK,), TOK_DEV // 4, TOK_DEV + 1)
    place = jax.random.randint(second, (), 0, NCHUNK)
    return jnp.where(jnp.arange(NCHUNK) == place, TOK_DEV, drawn).astype(jnp.int32)


def level_of(key, extent, cuts, smallest, high):
    def one(axis_at, shards_of):
        heights = jax.random.uniform(jax.random.fold_in(jax.random.fold_in(key, 6), axis_at), (shards_of,), jnp.float32, smallest / len(cuts), high / len(cuts))
        return jnp.repeat(jnp.exp(heights), extent[axis_at] // shards_of).reshape((-1,) + (1,) * (len(extent) - axis_at - 1))

    level = one(*cuts[0])
    for cut in cuts[1:]:
        level = level * one(*cut)
    return level


def gaussian(key, shape, scale, bound, shards=(), held_as=jnp.bfloat16):
    values = jax.random.normal(key, shape, jnp.float32) * scale
    if len(shards) > 0:
        values = level_of(key, shape, shards, -0.22, 0.18) * values
    return jnp.clip(values, min=-bound, max=bound).astype(held_as)


def setup_inputs(seed: int = 0) -> dict:
    seeds = jax.random.split(jax.random.key(seed), 10)
    queries = draw_queries(jax.random.fold_in(seeds[9], 71), 0)
    keys = draw_keys(jax.random.fold_in(seeds[9], 71), 0)
    values = gaussian(seeds[2], (TOKENS, D), 1.0, 6.0, ((0, 32), (1, 8)))
    window = draw_window(jax.random.fold_in(seeds[9], 71), 0)
    counts = draw_counts(jax.random.fold_in(seeds[9], 71), 0)
    gain = jnp.clip(1.0 + 0.1 * jax.random.normal(seeds[5], (D,), jnp.float32), 0.5, 1.5)
    w_gate = gaussian(seeds[6], (D, FFW), D ** -0.5, 0.078125, ((0, 8), (1, 32)))
    w_up = gaussian(seeds[7], (D, FFW), D ** -0.5, 0.078125, ((0, 8), (1, 32)))
    w_down = gaussian(seeds[8], (FFW, D), FFW ** -0.5, 0.046875, ((0, 32), (1, 8)))
    return dict(queries=queries, keys=keys, values=values, window=window, counts=counts, gain=gain, w_gate=w_gate, w_up=w_up, w_down=w_down)


def reference(queries, keys, values, window, counts, gain, w_gate, w_up, w_down):
    scale = HD ** (-0.5)
    query_blocks = queries.reshape(NCHUNK, TOK_DEV, HEADS, HD)
    pad_rows = jnp.zeros((WMAX * TOK_DEV, D), jnp.bfloat16)
    key_blocks = jnp.concatenate([pad_rows, keys], 0).reshape(NCHUNK + WMAX, TOK_DEV, HEADS, HD)
    value_blocks = jnp.concatenate([pad_rows, values], 0).reshape(NCHUNK + WMAX, TOK_DEV, HEADS, HD)
    padded_counts = jnp.concatenate([jnp.zeros((WMAX,), jnp.int32), counts])
    distance = WMAX - jnp.arange(WMAX + 1, dtype=jnp.int32)
    slots = jnp.arange(TOK_DEV, dtype=jnp.int32)

    def one_group(group):
        start = group.astype(jnp.int32)
        kc = lax.dynamic_slice_in_dim(key_blocks, start, WMAX + 1, 0).reshape((WMAX + 1) * TOK_DEV, HEADS, HD)
        vc = lax.dynamic_slice_in_dim(value_blocks, start, WMAX + 1, 0).reshape((WMAX + 1) * TOK_DEV, HEADS, HD)
        cc = lax.dynamic_slice_in_dim(padded_counts, start, WMAX + 1, 0)
        seen = (distance == 0) | (distance <= window[group]) & (group - distance >= 0)
        visible = (seen[:, None] & (slots[None, :] < cc[:, None])).reshape(-1)
        qc = query_blocks[group]
        scores = jnp.einsum('qhd,khd->hqk', qc.astype(jnp.float32), kc.astype(jnp.float32)) * scale
        scores = jnp.where(visible[None, None, :], scores, -1e+30)
        top = lax.optimization_barrier(jnp.max(scores, axis=-1, keepdims=True))
        expo = jnp.exp(scores - top)
        probs = (expo / lax.optimization_barrier(jnp.sum(expo, axis=-1, keepdims=True))).astype(jnp.bfloat16)
        attended = jnp.einsum('hqk,khd->qhd', probs.astype(jnp.float32), vc.astype(jnp.float32))
        return attended.reshape(TOK_DEV, D)
    attended = lax.map(one_group, jnp.arange(NCHUNK, dtype=jnp.int32)).reshape(TOKENS, D)
    meansq = lax.optimization_barrier(jnp.mean(attended * attended, axis=1, keepdims=True))
    normed = (attended * lax.rsqrt(meansq + 1e-06) * gain[None, :]).astype(jnp.bfloat16)
    both = jnp.concatenate([w_gate, w_up], 1)
    width = D // N_MP
    gate_up = jnp.zeros((TOKENS, 2 * FFW), jnp.float32)
    for part in range(N_MP):
        term = jnp.dot(normed[:, part * width:(part + 1) * width], both[part * width:(part + 1) * width], preferred_element_type=jnp.float32)
        gate_up = gate_up + lax.optimization_barrier(term.astype(jnp.bfloat16)).astype(jnp.float32)
    hidden = (jax.nn.silu(gate_up[:, :FFW]) * gate_up[:, FFW:]).astype(jnp.bfloat16)
    slab = FFW // N_TM

    def add_slab(index, total):
        first = (index * slab).astype(jnp.int32)
        rows = lax.dynamic_slice_in_dim(hidden, first, slab, 1)
        weights = lax.dynamic_slice_in_dim(w_down, first, slab, 0)
        term = jnp.dot(rows, weights, preferred_element_type=jnp.float32)
        return total + lax.optimization_barrier(term.astype(jnp.bfloat16)).astype(jnp.float32)
    ffn = lax.fori_loop(0, N_TM, add_slab, jnp.zeros((TOKENS, D), jnp.float32))
    return (normed.astype(jnp.float32) + ffn).astype(jnp.bfloat16)
```

```python
import functools

import jax
import jax.numpy as jnp
from jax import lax
from jax.experimental import pallas as pl
from jax.experimental.pallas import tpu as pltpu
from jax.sharding import PartitionSpec as P

MESH = pl.DeviceIdType.MESH
HD = 128
D = 6144
WMAX = 4
TOK = 128
HALF = 64
WID = 768
HID = 512
NX = 4
NZ = 8
SPLITS = ((0, 32), (32, 32))
SLOT = {0: 0, 1: 1, -1: 2, 2: 3, -2: 4, 3: 5, -3: 6, 4: 7}
GROUPS = ((0, 1), (1, 2), (3, 2), (5, 2), (7, 1))


def body(
    q_hbm, k_hbm, v_hbm, win_ref, cnt_ref, gain_ref, wg_hbm, wu_hbm, wd_hbm, out_ref, *scratch
):
    (q_ref, k_ref, v_ref, cn_ref, s_ref, att_ref, ss_ref, nrm_ref, wgu_ref, wd_ref) = scratch[:10]
    (x_refs, ps_refs, pr_refs, h_refs, os_refs, oc_refs, oo_refs, rs_refs, rr_refs, f_refs) = scratch[10:20]
    (load_sem, kv_send, kv_recv, w_send, w_recv, ss_send, ss_recv) = scratch[20:27]
    (y_sem, ag_sem, rl_sem, p_sem, h_sem, o_sem, r_sem, f_sem) = scratch[27:35]

    tm = lax.axis_index("tm")
    mp = lax.axis_index("mp")
    yl, z, c = tm // 16, (tm // 2) % NZ, tm % 2
    x, yh = mp // 2, mp % 2

    def dev(yl_=yl, z_=z, c_=c, x_=x, yh_=yh):
        return (yl_ * 16 + z_ * 2 + c_, x_ * 2 + yh_)

    z_up, z_down = lax.rem(z + 1, NZ), lax.rem(z + NZ - 1, NZ)
    core = dev(c_=1 - c)
    y_l, y_h, y_lh = dev(yl_=1 - yl), dev(yh_=1 - yh), dev(yl_=1 - yl, yh_=1 - yh)
    ups = (dev(z_=z_up), dev(z_=z_down))
    xs = [lax.rem(x + j, NX) for j in range(NX)]
    x_dev = [dev(x_=xs[j]) for j in range(NX)]
    xh_dev = [dev(x_=xs[j], yh_=1 - yh) for j in range(NX)]
    next_chip = (lax.rem(tm + 2, 32), mp)
    prev_chip = (lax.rem(tm + 30, 32), mp)

    sent = []

    def remote(src, dst, send_sem, recv_sem, device):
        copy = pltpu.make_async_remote_copy(
            src_ref=src, dst_ref=dst, send_sem=send_sem, recv_sem=recv_sem,
            device_id=device, device_id_type=MESH,
        )
        copy.start()
        sent.append(copy)
        return copy

    loads = []
    for i, (src, dst) in enumerate((
        (k_hbm, k_ref.at[0]), (v_hbm, v_ref.at[0]), (q_hbm, q_ref),
        (wg_hbm, wgu_ref.at[0, :, pl.ds(0, HID)]), (wu_hbm, wgu_ref.at[0, :, pl.ds(HID, HID)]),
        (wd_hbm, wd_ref.at[0]),
    )):
        copy = pltpu.make_async_copy(src, dst, load_sem.at[i])
        copy.start()
        loads.append(copy)

    cn_ref[0] = jnp.full((8, 128), cnt_ref[0], jnp.int32)

    barrier = pltpu.get_barrier_semaphore()
    partners = (core, y_l, y_h, y_lh, *ups, *x_dev[1:], *xh_dev[1:], next_chip, prev_chip)
    for device in partners:
        pl.semaphore_signal(barrier, inc=1, device_id=device, device_id_type=MESH)
    pl.semaphore_wait(barrier, len(partners))

    kv = (cn_ref, k_ref, v_ref)

    def kv_copy(i, src, dst, sem, device):
        return remote(kv[i].at[src], kv[i].at[dst], kv_send.at[sem, i], kv_recv.at[sem, i], device)

    loads[0].wait()
    loads[1].wait()
    own = [kv_copy(i, 0, 2, 0, next_chip) for i in range(3)]
    w_copies = [
        remote(wg_hbm, wgu_ref.at[1, :, pl.ds(0, HID)], w_send.at[0], w_recv.at[0], y_h),
        remote(wu_hbm, wgu_ref.at[1, :, pl.ds(HID, HID)], w_send.at[1], w_recv.at[1], y_h),
        remote(wd_hbm, wd_ref.at[1], w_send.at[2], w_recv.at[2], y_h),
    ]
    loads[2].wait()

    keys_at = lax.broadcasted_iota(jnp.int32, (1, TOK), 1)
    window = jnp.full((1, TOK), win_ref[0], jnp.int32)
    place = jnp.full((1, TOK), tm, jnp.int32)

    def score(e):
        visible = keys_at < cn_ref[e, 0:1, :]
        if e > 0:
            visible = visible & (window >= e) & (place >= e)
        for h in range(WID // HD):
            cols = pl.ds(h * HD, HD)
            s = lax.dot_general(
                q_ref[:, cols], k_ref[e, :, cols], (((1,), (1,)), ((), ())),
                preferred_element_type=jnp.float32,
            ) * HD ** (-0.5)
            s_ref[h, :, pl.ds(e * TOK, TOK)] = jnp.where(visible, s, -1e30)

    score(0)
    far, near, mid = [], [], []
    for i in range(3):
        own[i].wait_recv()
        far.append(kv_copy(i, 2, 4, 1, next_chip))
        near.append(kv_copy(i, 2 * c, 1, 2, core))
    score(2)
    for i in range(3):
        near[i].wait_recv()
    score(1)
    for i in range(3):
        far[i].wait_recv()
        mid.append(kv_copy(i, 2 * c + 2, 3, 3, core))
    score(4)
    for i in range(3):
        mid[i].wait_recv()
    score(3)

    squares = jnp.zeros((TOK, HD), jnp.float32)
    for h in range(WID // HD):
        cols = pl.ds(h * HD, HD)
        s = s_ref[h]
        expo = jnp.exp(s - jnp.max(s, axis=-1, keepdims=True))
        total = jnp.sum(expo, axis=-1, keepdims=True)
        vals = v_ref[:, :, cols].reshape((WMAX + 1) * TOK, HD)
        att = jnp.dot(expo.astype(jnp.bfloat16), vals, preferred_element_type=jnp.float32) / total
        att_ref[:, cols] = att
        squares = squares + att * att
    row = jnp.broadcast_to(jnp.sum(squares, axis=1, keepdims=True), (TOK, TOK))
    ss_ref[0] = jnp.transpose(row)[0:8]
    ss_copies = [
        remote(ss_ref.at[0], ss_ref.at[j], ss_send.at[j], ss_recv.at[j], device)
        for j, device in enumerate((y_h, *x_dev[1:], *xh_dev[1:]), start=1)
    ]
    for copy in ss_copies:
        copy.wait_recv()
    total = ss_ref[0]
    for j in range(1, 8):
        total = total + ss_ref[j]
    factor = lax.rsqrt(total / D + 1e-06)
    factor = jnp.transpose(jnp.broadcast_to(factor[0:1], (TOK, TOK)))
    for h in range(WID // HD):
        cols = pl.ds(h * HD, HD)
        normed = (att_ref[:, cols] * factor * gain_ref[:, cols]).astype(jnp.bfloat16)
        nrm_ref[:, :, cols] = normed.reshape(2, HALF, HD)

    y_copies = []
    for i, (off, size) in enumerate(SPLITS):
        rows = pl.ds(off, size)
        x_refs[i][0, 0, 0, 0] = nrm_ref[yh, rows]
        y_copies.append([
            remote(nrm_ref.at[1 - yh, rows], x_refs[i].at[0, 0, 1, 0], y_sem.at[0, i, 0], y_sem.at[1, i, 0], y_h),
            remote(nrm_ref.at[yh, rows], x_refs[i].at[0, 0, 0, 1], y_sem.at[0, i, 1], y_sem.at[1, i, 1], y_l),
            remote(nrm_ref.at[1 - yh, rows], x_refs[i].at[0, 0, 1, 1], y_sem.at[0, i, 2], y_sem.at[1, i, 2], y_lh),
        ])

    ring, relay = {}, {}

    def ring_send(i, way, m):
        sign = (-1, 1)[way]
        src = 0 if m == 1 else SLOT[sign * (m - 1)]
        dst = SLOT[4 if m == 4 else sign * m]
        src_ref, dst_ref = x_refs[i].at[src, 0], x_refs[i].at[dst, 0]
        if m == 4:
            src_ref, dst_ref = src_ref.at[way], dst_ref.at[way]
        ring[i, way, m] = remote(
            src_ref, dst_ref, ag_sem.at[0, i, way, m - 1], ag_sem.at[1, i, way, m - 1], ups[way]
        )

    def relay_send(i, slot):
        relay[i, slot] = remote(
            x_refs[i].at[slot, 0], x_refs[i].at[slot, 1], rl_sem.at[0, i, slot], rl_sem.at[1, i, slot], core
        )

    def gather(i, m):
        if m == 0:
            for copy in y_copies[i]:
                copy.wait_recv()
            ring_send(i, 0, 1)
            ring_send(i, 1, 1)
            relay_send(i, 0)
            return
        for way in range(2):
            ring[i, way, m].wait_recv()
            if m < 4:
                ring_send(i, way, m + 1)
                relay_send(i, SLOT[(-1, 1)[way] * m])
        if m == 4:
            relay_send(i, SLOT[4])

    p_copies, h_copies, o_copies, r_copies, f_copies = {}, {}, {}, {}, {}

    def gate_up(i, m):
        slot, count = GROUPS[m]
        size = SPLITS[i][1]
        for k in range(slot, slot + count):
            relay[i, k].wait_recv()
        for n in range(0, 2 * HID, 256):
            acc = None
            for half in range(2):
                tokens = x_refs[i][slot : slot + count, :, half].reshape(count * 4 * size, WID)
                part = jnp.dot(tokens, wgu_ref[half, :, n : n + 256], preferred_element_type=jnp.float32)
                acc = part if acc is None else acc + part
            ps_refs[i][slot : slot + count, :, :, n : n + 256] = acc.astype(jnp.bfloat16).reshape(
                count, 4, size, 256
            )
        p_copies[i, m] = [
            remote(
                ps_refs[i].at[pl.ds(slot, count), xs[j]], pr_refs[i].at[pl.ds(slot, count), j - 1],
                p_sem.at[0, i, m, j - 1], p_sem.at[1, i, m, j - 1], x_dev[j],
            )
            for j in (2, 1, 3)
        ]

    def hidden(i, m):
        slot, count = GROUPS[m]
        for copy in p_copies[i, m]:
            copy.wait_recv()
        for k in range(slot, slot + count):
            both = ps_refs[i][k, x].astype(jnp.float32)
            for j in range(NX - 1):
                both = both + pr_refs[i][k, j].astype(jnp.float32)
            gate, up = both[:, :HID], both[:, HID:]
            h_refs[i][k, x] = (gate / (1.0 + jnp.exp(-gate)) * up).astype(jnp.bfloat16)
        ref = h_refs[i].at[pl.ds(slot, count), x]
        h_copies[i, m] = [
            remote(ref, ref, h_sem.at[0, i, m, j - 1], h_sem.at[1, i, m, j - 1], x_dev[j]) for j in (2, 1, 3)
        ]

    def down(i, m):
        slot, count = GROUPS[m]
        size = SPLITS[i][1]
        for copy in h_copies[i, m]:
            copy.wait_recv()
        rows = h_refs[i][slot : slot + count].reshape(count * 4 * size, HID)
        for half in range(2):
            for n in range(0, WID, 256):
                o = jnp.dot(rows, wd_ref[half, :, n : n + 256], preferred_element_type=jnp.float32)
                o = o.reshape(count, 2, 2, size, 256)
                oo_refs[i][slot : slot + count, half, :, :, n : n + 256] = o[:, 0]
                os_refs[i][slot : slot + count, half, :, :, n : n + 256] = o[:, 1].astype(jnp.bfloat16)
        o_copies[i, m] = remote(
            os_refs[i].at[pl.ds(slot, count)], oc_refs[i].at[pl.ds(slot, count)],
            o_sem.at[0, i, m], o_sem.at[1, i, m], core,
        )

    def both_cores(i, m):
        slot, count = GROUPS[m]
        o_copies[i, m].wait_recv()
        for k in range(slot, slot + count):
            oo_refs[i][k] += oc_refs[i][k].astype(jnp.float32)

    def sums(i, r):
        for way in range(2):
            sign = (1, -1)[way]
            if r == 0:
                rs_refs[i][way, 0, 0] = oo_refs[i][SLOT[4], way].astype(jnp.bfloat16)
                src, dst = rs_refs[i].at[way, 0, 0], rr_refs[i].at[way, 0, way]
            else:
                r_copies[i, way, r - 1].wait_recv()
                slot = SLOT[sign * (4 - r)]
                if r == 1:
                    rs_refs[i][way, 1, way] = (
                        oo_refs[i][slot, way] + rr_refs[i][way, 0, way].astype(jnp.float32)
                    ).astype(jnp.bfloat16)
                    rs_refs[i][way, 1, 1 - way] = oo_refs[i][slot, 1 - way].astype(jnp.bfloat16)
                else:
                    rs_refs[i][way, r] = (
                        oo_refs[i][slot] + rr_refs[i][way, r - 1].astype(jnp.float32)
                    ).astype(jnp.bfloat16)
                src, dst = rs_refs[i].at[way, r], rr_refs[i].at[way, r]
            r_copies[i, way, r] = remote(src, dst, r_sem.at[0, i, way, r], r_sem.at[1, i, way, r], ups[way])

    def deliver(i):
        for way in range(2):
            r_copies[i, way, 3].wait_recv()
        ref = oo_refs[i]
        own = rr_refs[i]
        ref[0] += own[0, 3].astype(jnp.float32) + own[1, 3].astype(jnp.float32)
        for j, (half, group, device) in enumerate(((0, 1, y_l), (1, 0, y_h), (1, 1, y_lh))):
            f_refs[i][0, j] = ref[0, half, group].astype(jnp.bfloat16)
            f_copies[i, j] = remote(
                f_refs[i].at[0, j], f_refs[i].at[1, j], f_sem.at[0, i, j], f_sem.at[1, i, j], device
            )

    def finish(i):
        off, size = SPLITS[i]
        rows = pl.ds(off, size)
        for j in range(3):
            f_copies[i, j].wait_recv()
        got = f_refs[i]
        mine = oo_refs[i][0, 0, 0] + got[1, 0].astype(jnp.float32)
        theirs = got[1, 1].astype(jnp.float32) + got[1, 2].astype(jnp.float32)
        out_ref[yh, rows] = (nrm_ref[yh, rows].astype(jnp.float32) + mine).astype(jnp.bfloat16)
        out_ref[1 - yh, rows] = (nrm_ref[1 - yh, rows].astype(jnp.float32) + theirs).astype(jnp.bfloat16)

    steps = [(i, m) for i in range(len(SPLITS)) for m in range(len(GROUPS))]
    for i in range(len(SPLITS)):
        gather(i, 0)
    for copy in loads[3:]:
        copy.wait()
    for copy in w_copies[:2]:
        copy.wait_recv()
    tail = []
    for k in range(len(steps) + 3):
        if k < len(steps):
            gate_up(*steps[k])
        if k + 1 < len(steps) and steps[k + 1][1] > 0:
            gather(*steps[k + 1])
        if 0 <= k - 1 < len(steps):
            hidden(*steps[k - 1])
        if 0 <= k - 2 < len(steps):
            if k == 2:
                w_copies[2].wait_recv()
            down(*steps[k - 2])
        if 0 <= k - 3 < len(steps):
            i, m = steps[k - 3]
            both_cores(i, m)
            if m == len(GROUPS) - 1:
                tail += [functools.partial(sums, i, r) for r in range(4)]
                tail += [functools.partial(deliver, i), functools.partial(finish, i)]
        if tail:
            tail.pop(0)()
    for part in tail:
        part()

    for copy in sent:
        copy.wait_send()


def per_device(queries, keys, values, window, counts, gain, w_gate, w_up, w_down):
    bf, f32 = jnp.bfloat16, jnp.float32
    n = len(SPLITS)
    sizes = [size for _, size in SPLITS]

    def each(shape_of, dtype):
        return [pltpu.VMEM(shape_of(size), dtype) for size in sizes]

    dma = pltpu.SemaphoreType.DMA
    steps = len(GROUPS)
    scratch = [
        pltpu.VMEM((TOK, WID), bf),
        pltpu.VMEM((WMAX + 1, TOK, WID), bf),
        pltpu.VMEM((WMAX + 1, TOK, WID), bf),
        pltpu.VMEM((WMAX + 1, 8, 128), jnp.int32),
        pltpu.VMEM((WID // HD, TOK, (WMAX + 1) * TOK), f32),
        pltpu.VMEM((TOK, WID), f32),
        pltpu.VMEM((8, 8, 128), f32),
        pltpu.VMEM((2, HALF, WID), bf),
        pltpu.VMEM((2, WID, 2 * HID), bf),
        pltpu.VMEM((2, HID, WID), bf),
        each(lambda s: (NZ, 2, 2, 2, s, WID), bf),
        each(lambda s: (NZ, NX, s, 2 * HID), bf),
        each(lambda s: (NZ, NX - 1, s, 2 * HID), bf),
        each(lambda s: (NZ, NX, s, HID), bf),
        each(lambda s: (NZ, 2, 2, s, WID), bf),
        each(lambda s: (NZ, 2, 2, s, WID), bf),
        each(lambda s: (NZ, 2, 2, s, WID), f32),
        each(lambda s: (2, 4, 2, 2, s, WID), bf),
        each(lambda s: (2, 4, 2, 2, s, WID), bf),
        each(lambda s: (2, 3, s, WID), bf),
        dma((6,)), dma((4, 3)), dma((4, 3)), dma((3,)), dma((3,)), dma((8,)), dma((8,)),
        dma((2, n, 3)), dma((2, n, 2, 4)), dma((2, n, NZ)), dma((2, n, steps, 3)), dma((2, n, steps, 3)),
        dma((2, n, steps)), dma((2, n, 2, 4)), dma((2, n, 3)),
    ]
    hbm = pl.BlockSpec(memory_space=pl.ANY)
    smem = pl.BlockSpec(memory_space=pltpu.SMEM)
    vmem = pl.BlockSpec(memory_space=pltpu.VMEM)
    out = pl.pallas_call(
        body,
        out_shape=jax.ShapeDtypeStruct((2, HALF, WID), bf),
        in_specs=[hbm, hbm, hbm, smem, smem, vmem, hbm, hbm, hbm],
        out_specs=vmem,
        scratch_shapes=scratch,
        compiler_params=pltpu.CompilerParams(
            collective_id=0, has_side_effects=True, vmem_limit_bytes=60 * 2**20
        ),
        cost_estimate=pl.CostEstimate(flops=10**10, bytes_accessed=3 * 10**6, transcendentals=10**6),
        name="block",
    )(queries, keys, values, window, counts, gain.reshape(1, WID), w_gate, w_up, w_down)
    return out.reshape(TOK, WID)


def solution(mesh):
    in_specs = (
        P("tm", "mp"),
        P("tm", "mp"),
        P("tm", "mp"),
        P("tm"),
        P("tm"),
        P("mp"),
        P("mp", "tm"),
        P("mp", "tm"),
        P("tm", "mp"),
    )
    return jax.shard_map(
        per_device, mesh=mesh, in_specs=in_specs, out_specs=P("tm", "mp"), check_vma=False
    )
```

```python
import functools

import jax
import jax.numpy as jnp
from jax import lax
from jax.experimental import pallas as pl
from jax.experimental.pallas import tpu as pltpu
from jax.sharding import PartitionSpec as P

MESH = pl.DeviceIdType.MESH
HD = 128
D = 6144
WMAX = 4
TOK = 128
HALF = 64
WID = 768
HID = 512
QUART = 256
NX = 4
NZ = 8
SPLITS = ((0, 16), (16, 16), (32, 16), (48, 16))
SLOT = {0: 0, 1: 1, -1: 2, 2: 3, -2: 4, 3: 5, -3: 6, 4: 7}
GROUPS = ((0, 1), (1, 2), (3, 2), (5, 2), (7, 1))
STEPS = tuple((i, m) for m in range(5) for i in (0, 1)) + tuple((i, 4 - m) for m in range(5) for i in (2, 3))
LAGS = (0, 1, 2, 3, 5, 6)
GATHERS = ((None, 1, 3, 4, 7), (0, 2, 3, 5, 8), (1, 3, 6, 8, 9), (1, 4, 7, 8, 10))
EARLY = 2
HOLD = ((0, 3, 3, 1, 0, 2), (0, 3, 2, 2, 2, 1), (1, 1, 0, 0, 1, 2), (0, 0, 0, 0, 2, 2))


def body(
    q_hbm, k_hbm, v_hbm, win_ref, cnt_ref, gain_ref, wg_hbm, wu_hbm, wd_hbm, out_ref, *scratch
):
    (q_ref, k_ref, v_ref, cn_ref, s_ref, att_ref, ss_ref, nrm_ref, wgu_ref, wd_ref) = scratch[:10]
    (x_refs, ps_refs, pa_refs, pr_refs, h_refs, os_refs, oc_refs, oo_refs, rs_refs, rr_refs, f_refs) = scratch[10:21]
    (load_sem, kv_send, kv_recv, w_send, w_recv, ss_send, ss_recv) = scratch[21:28]
    (y_sem, ag_sem, rl_sem, pa_sem, p_sem, h_sem, hf_sem, o_sem, r_sem, f_sem) = scratch[28:38]

    tm = lax.axis_index("tm")
    mp = lax.axis_index("mp")
    yl, z, c = tm // 16, (tm // 2) % NZ, tm % 2
    x, yh = mp // 2, mp % 2

    def dev(yl_=yl, z_=z, c_=c, x_=x, yh_=yh):
        return (yl_ * 16 + z_ * 2 + c_, x_ * 2 + yh_)

    z_up, z_down = lax.rem(z + 1, NZ), lax.rem(z + NZ - 1, NZ)
    core = dev(c_=1 - c)
    y_l, y_h = dev(yl_=1 - yl), dev(yh_=1 - yh)
    ups = (dev(z_=z_up), dev(z_=z_down))
    xs = [lax.rem(x + j, NX) for j in range(NX)]
    x_dev = [dev(x_=xs[j]) for j in range(NX)]
    xh_dev = [dev(x_=xs[j], yh_=1 - yh) for j in range(NX)]
    mate, mate_l = dev(x_=x + 1 - 2 * (x % 2)), dev(x_=x + 1 - 2 * (x % 2), yl_=1 - yl)
    th = ((x + 1) // 2) % 2
    xa = x // 2
    across = (dev(x_=3 - x), y_h)
    next_chip = (lax.rem(tm + 2, 32), mp)
    prev_chip = (lax.rem(tm + 30, 32), mp)

    sent = []

    def remote(src, dst, send_sem, recv_sem, device):
        copy = pltpu.make_async_remote_copy(
            src_ref=src, dst_ref=dst, send_sem=send_sem, recv_sem=recv_sem,
            device_id=device, device_id_type=MESH,
        )
        copy.start()
        sent.append(copy)
        return copy

    loads = []
    for i, (src, dst) in enumerate((
        (k_hbm, k_ref.at[0]), (v_hbm, v_ref.at[0]), (q_hbm, q_ref),
        (wd_hbm, wd_ref.at[0]),
        *((w.at[:, pl.ds(half * QUART, QUART)], wgu_ref.at[0, :, pl.ds((2 * half + j) * QUART, QUART)])
          for half in range(2) for j, w in enumerate((wg_hbm, wu_hbm))),
    )):
        copy = pltpu.make_async_copy(src, dst, load_sem.at[i])
        copy.start()
        loads.append(copy)

    cn_ref[0] = jnp.full((8, 128), cnt_ref[0], jnp.int32)

    barrier = pltpu.get_barrier_semaphore()
    partners = (core, y_l, y_h, mate_l, *ups, *x_dev[1:], *xh_dev[1:], next_chip, prev_chip)
    for device in partners:
        pl.semaphore_signal(barrier, inc=1, device_id=device, device_id_type=MESH)
    pl.semaphore_wait(barrier, len(partners))

    kv = (cn_ref, k_ref, v_ref)

    def kv_copy(i, src, dst, sem, device):
        return remote(kv[i].at[src], kv[i].at[dst], kv_send.at[sem, i], kv_recv.at[sem, i], device)

    loads[0].wait()
    loads[1].wait()
    own = [kv_copy(i, 0, 2, 0, next_chip) for i in range(3)]
    w_copies = [
        remote(
            w.at[:, pl.ds(half * QUART, QUART)], wgu_ref.at[1, :, pl.ds((2 * half + j) * QUART, QUART)],
            w_send.at[2 * half + j], w_recv.at[2 * half + j], mate,
        )
        for half in range(2) for j, w in enumerate((wg_hbm, wu_hbm))
    ]
    loads[2].wait()

    keys_at = lax.broadcasted_iota(jnp.int32, (1, TOK), 1)
    window = jnp.full((1, TOK), win_ref[0], jnp.int32)
    place = jnp.full((1, TOK), tm, jnp.int32)

    def score(e):
        visible = keys_at < cn_ref[e, 0:1, :]
        if e > 0:
            visible = visible & (window >= e) & (place >= e)
        for h in range(WID // HD):
            cols = pl.ds(h * HD, HD)
            s = lax.dot_general(
                q_ref[:, cols], k_ref[e, :, cols], (((1,), (1,)), ((), ())),
                preferred_element_type=jnp.float32,
            ) * HD ** (-0.5)
            s_ref[h, :, pl.ds(e * TOK, TOK)] = jnp.where(visible, s, -1e30)

    score(0)
    far, near, mid = [], [], []
    for i in range(3):
        own[i].wait_recv()
        far.append(kv_copy(i, 2, 4, 1, next_chip))
        near.append(kv_copy(i, 2 * c, 1, 2, core))
    score(2)
    for i in range(3):
        near[i].wait_recv()
    score(1)
    for i in range(3):
        far[i].wait_recv()
        mid.append(kv_copy(i, 2 * c + 2, 3, 3, core))
    score(4)
    for i in range(3):
        mid[i].wait_recv()
    score(3)

    squares = jnp.zeros((TOK, HD), jnp.float32)
    for h in range(WID // HD):
        cols = pl.ds(h * HD, HD)
        s = s_ref[h]
        expo = jnp.exp(s - jnp.max(s, axis=-1, keepdims=True))
        total = jnp.sum(expo, axis=-1, keepdims=True)
        vals = v_ref[:, :, cols].reshape((WMAX + 1) * TOK, HD)
        att = jnp.dot(expo.astype(jnp.bfloat16), vals, preferred_element_type=jnp.float32) / total
        att_ref[:, cols] = att
        squares = squares + att * att
    row = jnp.broadcast_to(jnp.sum(squares, axis=1, keepdims=True), (TOK, TOK))
    ss_ref[0] = jnp.transpose(row)[0:8]
    ss_copies = [
        remote(ss_ref.at[0], ss_ref.at[j], ss_send.at[j], ss_recv.at[j], device)
        for j, device in enumerate((y_h, *x_dev[1:], *xh_dev[1:]), start=1)
    ]
    for copy in ss_copies:
        copy.wait_recv()
    total = ss_ref[0]
    for j in range(1, 8):
        total = total + ss_ref[j]
    factor = lax.rsqrt(total / D + 1e-06)
    factor = jnp.transpose(jnp.broadcast_to(factor[0:1], (TOK, TOK)))
    for h in range(WID // HD):
        cols = pl.ds(h * HD, HD)
        normed = (att_ref[:, cols] * factor * gain_ref[:, cols]).astype(jnp.bfloat16)
        nrm_ref[:, :, cols] = normed.reshape(2, HALF, HD)

    y_copies = []

    def spread(i):
        off, size = SPLITS[i]
        rows = pl.ds(off, size)
        x_refs[i][0, 0, 0, 0] = nrm_ref[th, rows]
        y_copies.append([
            remote(nrm_ref.at[1 - th, rows], x_refs[i].at[0, 0, 1, 0], y_sem.at[0, i, 0], y_sem.at[1, i, 0], mate),
            remote(nrm_ref.at[th, rows], x_refs[i].at[0, 0, 0, 1], y_sem.at[0, i, 1], y_sem.at[1, i, 1], y_l),
            remote(nrm_ref.at[1 - th, rows], x_refs[i].at[0, 0, 1, 1], y_sem.at[0, i, 2], y_sem.at[1, i, 2], mate_l),
        ])

    ring, relay = {}, {}

    def ring_send(i, way, m):
        sign = (-1, 1)[way]
        src = 0 if m == 1 else SLOT[sign * (m - 1)]
        dst = SLOT[4 if m == 4 else sign * m]
        src_ref, dst_ref = x_refs[i].at[src, 0], x_refs[i].at[dst, 0]
        if m == 4:
            src_ref, dst_ref = src_ref.at[way], dst_ref.at[way]
        ring[i, way, m] = remote(
            src_ref, dst_ref, ag_sem.at[0, i, way, m - 1], ag_sem.at[1, i, way, m - 1], ups[way]
        )

    def relay_send(i, slot):
        relay[i, slot] = remote(
            x_refs[i].at[slot, 0], x_refs[i].at[slot, 1], rl_sem.at[0, i, slot], rl_sem.at[1, i, slot], core
        )

    def gather(i, m):
        if m == 0:
            for copy in y_copies[i]:
                copy.wait_recv()
            ring_send(i, 0, 1)
            ring_send(i, 1, 1)
            relay_send(i, 0)
            return
        for way in range(2):
            ring[i, way, m].wait_recv()
            if m < 4:
                ring_send(i, way, m + 1)
                relay_send(i, SLOT[(-1, 1)[way] * m])
        if m == 4:
            relay_send(i, SLOT[4])

    pa_copies, p_copies, h_copies, hf_copies, o_copies, r_copies, f_copies = {}, {}, {}, {}, {}, {}, {}

    def gate_up(i, m):
        slot, count = GROUPS[m]
        size = SPLITS[i][1]
        for k in range(slot, slot + count):
            relay[i, k].wait_recv()
        for n in range(0, 2 * HID, 256):
            acc = None
            for half in range(2):
                tokens = x_refs[i][slot : slot + count, :, half].reshape(count * 4 * size, WID)
                part = jnp.dot(tokens, wgu_ref[half, :, n : n + 256], preferred_element_type=jnp.float32)
                acc = part if acc is None else acc + part
            ps_refs[i][slot : slot + count, :, :, :, n : n + 256] = acc.astype(jnp.bfloat16).reshape(
                count, 2, 2, size, 256
            )
        slots = pl.ds(slot, count)
        out = (
            ps_refs[i].at[slots, 1 - xa, :, :, pl.ds(0, HID)],
            ps_refs[i].at[slots, :, 1 - yh, :, pl.ds(HID, HID)],
        )
        pa_copies[i, m] = [
            remote(
                out[way], pa_refs[i].at[slots, way], pa_sem.at[0, i, m, way], pa_sem.at[1, i, m, way], across[way]
            )
            for way in range(2)
        ]

    def combine(i, m):
        slot, count = GROUPS[m]
        slots = pl.ds(slot, count)
        p_copies[i, m] = []
        for way in range(2):
            pa_copies[i, m][way].wait_recv()
            cols = pl.ds(way * HID, HID)
            a, b = ((xa, 1 - yh), (1 - xa, yh))[way]
            for k in range(slot, slot + count):
                ps_refs[i][k, a, b, :, cols] = (
                    ps_refs[i][k, a, b, :, cols].astype(jnp.float32)
                    + pa_refs[i][k, way, (b, a)[way]].astype(jnp.float32)
                ).astype(jnp.bfloat16)
            p_copies[i, m].append(remote(
                ps_refs[i].at[slots, a, b, :, cols], pr_refs[i].at[slots, way],
                p_sem.at[0, i, m, way], p_sem.at[1, i, m, way], across[1 - way],
            ))

    def hidden(i, m):
        slot, count = GROUPS[m]
        slots = pl.ds(slot, count)
        h_copies[i, m] = []
        for way in range(2):
            p_copies[i, m][way].wait_recv()
            cols = pl.ds(way * QUART, QUART)
            for k in range(slot, slot + count):
                both = (
                    ps_refs[i][k, xa, yh, :, pl.ds(way * HID, HID)].astype(jnp.float32)
                    + pa_refs[i][k, way, (yh, xa)[way]].astype(jnp.float32)
                    + pr_refs[i][k, way].astype(jnp.float32)
                )
                gate, up = both[:, :QUART], both[:, QUART:]
                h_refs[i][k, xa, yh, :, cols] = (gate / (1.0 + jnp.exp(-gate)) * up).astype(jnp.bfloat16)
            ref = h_refs[i].at[slots, xa, yh, :, cols]
            h_copies[i, m].append(
                remote(ref, ref, h_sem.at[0, i, m, way], h_sem.at[1, i, m, way], across[1 - way])
            )

    def forward(i, m):
        slot, count = GROUPS[m]
        slots = pl.ds(slot, count)
        hf_copies[i, m] = []
        for way in range(2):
            h_copies[i, m][way].wait_recv()
            cols = pl.ds(way * QUART, QUART)
            ref = (h_refs[i].at[slots, xa, :, :, cols], h_refs[i].at[slots, :, yh, :, cols])[way]
            hf_copies[i, m].append(
                remote(ref, ref, hf_sem.at[0, i, m, way], hf_sem.at[1, i, m, way], across[way])
            )

    def down(i, m):
        slot, count = GROUPS[m]
        size = SPLITS[i][1]
        for copy in hf_copies[i, m]:
            copy.wait_recv()
        rows = h_refs[i][slot : slot + count].reshape(count * 4 * size, HID)
        for half in range(2):
            for n in range(0, WID, 256):
                o = jnp.dot(rows, wd_ref[half, :, n : n + 256], preferred_element_type=jnp.float32)
                o = o.reshape(count, 2, 2, size, 256)
                oo_refs[i][slot : slot + count, half, :, :, n : n + 256] = o[:, 0]
                os_refs[i][slot : slot + count, half, :, :, n : n + 256] = o[:, 1].astype(jnp.bfloat16)
        o_copies[i, m] = remote(
            os_refs[i].at[pl.ds(slot, count)], oc_refs[i].at[pl.ds(slot, count)],
            o_sem.at[0, i, m], o_sem.at[1, i, m], core,
        )

    def both_cores(i, m):
        slot, count = GROUPS[m]
        o_copies[i, m].wait_recv()
        for k in range(slot, slot + count):
            oo_refs[i][k] += oc_refs[i][k].astype(jnp.float32)

    def sums(i, r):
        for way in range(2):
            sign = (1, -1)[way]
            if r == 0:
                rs_refs[i][way, 0, 0] = oo_refs[i][SLOT[4], way].astype(jnp.bfloat16)
                src, dst = rs_refs[i].at[way, 0, 0], rr_refs[i].at[way, 0, way]
            else:
                r_copies[i, way, r - 1].wait_recv()
                slot = SLOT[sign * (4 - r)]
                if r == 1:
                    rs_refs[i][way, 1, way] = (
                        oo_refs[i][slot, way] + rr_refs[i][way, 0, way].astype(jnp.float32)
                    ).astype(jnp.bfloat16)
                    rs_refs[i][way, 1, 1 - way] = oo_refs[i][slot, 1 - way].astype(jnp.bfloat16)
                else:
                    rs_refs[i][way, r] = (
                        oo_refs[i][slot] + rr_refs[i][way, r - 1].astype(jnp.float32)
                    ).astype(jnp.bfloat16)
                src, dst = rs_refs[i].at[way, r], rr_refs[i].at[way, r]
            r_copies[i, way, r] = remote(src, dst, r_sem.at[0, i, way, r], r_sem.at[1, i, way, r], ups[way])

    def deliver(i):
        for way in range(2):
            r_copies[i, way, 3].wait_recv()
        ref = oo_refs[i]
        own = rr_refs[i]
        ref[0] += own[0, 3].astype(jnp.float32) + own[1, 3].astype(jnp.float32)
        for j, (half, group, device) in enumerate(((0, 1, y_l), (1, 0, mate), (1, 1, mate_l))):
            f_refs[i][0, j] = ref[0, half, group].astype(jnp.bfloat16)
            f_copies[i, j] = remote(
                f_refs[i].at[0, j], f_refs[i].at[1, j], f_sem.at[0, i, j], f_sem.at[1, i, j], device
            )

    def finish(i):
        off, size = SPLITS[i]
        rows = pl.ds(off, size)
        for j in range(3):
            f_copies[i, j].wait_recv()
        got = f_refs[i]
        mine = oo_refs[i][0, 0, 0] + got[1, 0].astype(jnp.float32)
        theirs = got[1, 1].astype(jnp.float32) + got[1, 2].astype(jnp.float32)
        out_ref[th, rows] = (nrm_ref[th, rows].astype(jnp.float32) + mine).astype(jnp.bfloat16)
        out_ref[1 - th, rows] = (nrm_ref[1 - th, rows].astype(jnp.float32) + theirs).astype(jnp.bfloat16)

    stages = (gate_up, combine, hidden, forward, down, both_cores)
    last = LAGS[-1]
    gathers = sorted(
        (at, i, m) for i, row in enumerate(GATHERS) for m, at in enumerate(row) if at is not None
    )
    tails = []
    for i, hold in enumerate(HOLD):
        at = 0
        for j in range(6):
            ready = last + STEPS.index((i, max(4 - j, 0)))
            at = max(at + 1 + (hold[j] if j > 3 else 0), ready + (hold[j] if j < 5 else 0))
            part = functools.partial(sums, i, j) if j < 4 else functools.partial((deliver, finish)[j - 4], i)
            tails.append((at, part))
    tails.sort(key=lambda t: t[0])

    def run_gathers(k):
        while gathers and gathers[0][0] <= k:
            gather(*gathers.pop(0)[1:])

    spread(0)
    gather(0, 0)
    for i in range(1, len(SPLITS)):
        spread(i)
    run_gathers(EARLY - 1)
    for copy in loads[3:]:
        copy.wait()
    for copy in w_copies:
        copy.wait_recv()
    w_copies.append(remote(wd_hbm, wd_ref.at[1], w_send.at[4], w_recv.at[4], mate))
    for k in range(len(STEPS) + last):
        for lag, stage in zip(LAGS, stages):
            if 0 <= k - lag < len(STEPS):
                if stage is down and k == lag:
                    w_copies[4].wait_recv()
                stage(*STEPS[k - lag])
            if lag == 0:
                run_gathers(k)
        while tails and tails[0][0] <= k:
            tails.pop(0)[1]()
    for _, part in tails:
        part()

    for copy in sent:
        copy.wait_send()


def per_device(queries, keys, values, window, counts, gain, w_gate, w_up, w_down):
    bf, f32 = jnp.bfloat16, jnp.float32
    n = len(SPLITS)
    sizes = [size for _, size in SPLITS]

    def each(shape_of, dtype):
        return [pltpu.VMEM(shape_of(size), dtype) for size in sizes]

    dma = pltpu.SemaphoreType.DMA
    steps = len(GROUPS)
    scratch = [
        pltpu.VMEM((TOK, WID), bf),
        pltpu.VMEM((WMAX + 1, TOK, WID), bf),
        pltpu.VMEM((WMAX + 1, TOK, WID), bf),
        pltpu.VMEM((WMAX + 1, 8, 128), jnp.int32),
        pltpu.VMEM((WID // HD, TOK, (WMAX + 1) * TOK), f32),
        pltpu.VMEM((TOK, WID), f32),
        pltpu.VMEM((8, 8, 128), f32),
        pltpu.VMEM((2, HALF, WID), bf),
        pltpu.VMEM((2, WID, 2 * HID), bf),
        pltpu.VMEM((2, HID, WID), bf),
        each(lambda s: (NZ, 2, 2, 2, s, WID), bf),
        each(lambda s: (NZ, 2, 2, s, 2 * HID), bf),
        each(lambda s: (NZ, 2, 2, s, HID), bf),
        each(lambda s: (NZ, 2, s, HID), bf),
        each(lambda s: (NZ, 2, 2, s, HID), bf),
        each(lambda s: (NZ, 2, 2, s, WID), bf),
        each(lambda s: (NZ, 2, 2, s, WID), bf),
        each(lambda s: (NZ, 2, 2, s, WID), f32),
        each(lambda s: (2, 4, 2, 2, s, WID), bf),
        each(lambda s: (2, 4, 2, 2, s, WID), bf),
        each(lambda s: (2, 3, s, WID), bf),
        dma((8,)), dma((4, 3)), dma((4, 3)), dma((5,)), dma((5,)), dma((8,)), dma((8,)),
        dma((2, n, 3)), dma((2, n, 2, 4)), dma((2, n, NZ)), dma((2, n, steps, 2)), dma((2, n, steps, 2)),
        dma((2, n, steps, 2)), dma((2, n, steps, 2)),
        dma((2, n, steps)), dma((2, n, 2, 4)), dma((2, n, 3)),
    ]
    hbm = pl.BlockSpec(memory_space=pl.ANY)
    smem = pl.BlockSpec(memory_space=pltpu.SMEM)
    vmem = pl.BlockSpec(memory_space=pltpu.VMEM)
    out = pl.pallas_call(
        body,
        out_shape=jax.ShapeDtypeStruct((2, HALF, WID), bf),
        in_specs=[hbm, hbm, hbm, smem, smem, vmem, hbm, hbm, hbm],
        out_specs=vmem,
        scratch_shapes=scratch,
        compiler_params=pltpu.CompilerParams(
            collective_id=0, has_side_effects=True, vmem_limit_bytes=60 * 2**20
        ),
        cost_estimate=pl.CostEstimate(flops=10**10, bytes_accessed=3 * 10**6, transcendentals=10**6),
        name="block",
    )(queries, keys, values, window, counts, gain.reshape(1, WID), w_gate, w_up, w_down)
    return out.reshape(TOK, WID)


def solution(mesh):
    in_specs = (
        P("tm", "mp"),
        P("tm", "mp"),
        P("tm", "mp"),
        P("tm"),
        P("tm"),
        P("mp"),
        P("mp", "tm"),
        P("mp", "tm"),
        P("tm", "mp"),
    )
    return jax.shard_map(
        per_device, mesh=mesh, in_specs=in_specs, out_specs=P("tm", "mp"), check_vma=False
    )
```

```python
import functools

import jax
import jax.numpy as jnp
from jax import lax
from jax.experimental import pallas as pl
from jax.experimental.pallas import tpu as pltpu
from jax.sharding import PartitionSpec as P

MESH = pl.DeviceIdType.MESH
HD = 128
D = 6144
WMAX = 4
TOK = 128
HALF = 64
WID = 768
HID = 512
QUART = 256
NX = 4
NZ = 8
SPLITS = ((0, 16), (16, 16), (32, 16), (48, 16))
NEAR = {0: 0, 1: 1, -1: 2, 2: 3, -2: 4, 3: 5, -3: 6, 4: 7}
FAR = {-1: 0, 0: 1, -2: 2, 1: 3, -3: 4, 2: 5, 4: 6, 3: 7}
SLOTS = (NEAR, NEAR, FAR, FAR)
GROUPS = ((0, 1), (1, 2), (3, 2), (5, 2), (7, 1))
STEPS = tuple((i, m) for m in range(5) for i in (0, 1)) + tuple((i, 4 - m) for m in range(5) for i in (2, 3))
LAGS = (0, 1, 2, 3, 4, 5)
GATHERS = ((None, 1, 3, 5, 6), (-13, 2, 4, 6, 7), (-10, 5, 6, 8, 10), (3, 5, 7, 9, 10))
EARLY = 0
SECOND, DOWN = 6, 10
HOLD = ((2, 2, 2, 1, 5, 4), (0, 2, 2, 2, 4, 2), (0, 1, 1, 0, 1, 7), (0, 1, 0, 0, 4, 5))


def body(
    q_hbm, k_hbm, v_hbm, win_ref, cnt_ref, gain_ref, wg_hbm, wu_hbm, wd_hbm, out_ref, *scratch
):
    (qo_ref, q_ref, k_ref, v_ref, cn_ref, s_ref, att_ref, ss_ref, nrm_ref, wgu_ref, wd_ref) = scratch[:11]
    (x_refs, ps_refs, pa_refs, pr_refs, h_refs, os_refs, oc_refs, oo_refs, rs_refs, rr_refs, f_refs) = scratch[11:22]
    (load_sem, kv_send, kv_recv, w_send, w_recv, ss_send, ss_recv) = scratch[22:29]
    (y_sem, ag_sem, rl_sem, pa_sem, p_sem, h_sem, hf_sem, o_sem, r_sem, f_sem) = scratch[29:39]

    tm = lax.axis_index("tm")
    mp = lax.axis_index("mp")
    yl, z, c = tm // 16, (tm // 2) % NZ, tm % 2
    x, yh = mp // 2, mp % 2

    def dev(yl_=yl, z_=z, c_=c, x_=x, yh_=yh):
        return (yl_ * 16 + z_ * 2 + c_, x_ * 2 + yh_)

    z_up, z_down = lax.rem(z + 1, NZ), lax.rem(z + NZ - 1, NZ)
    core = dev(c_=1 - c)
    y_l, y_h = dev(yl_=1 - yl), dev(yh_=1 - yh)
    ups = (dev(z_=z_up), dev(z_=z_down))
    xs = [lax.rem(x + j, NX) for j in range(NX)]
    x_dev = [dev(x_=xs[j]) for j in range(NX)]
    xh_dev = [dev(x_=xs[j], yh_=1 - yh) for j in range(NX)]
    mate, mate_l = dev(x_=x + 1 - 2 * (x % 2)), dev(x_=x + 1 - 2 * (x % 2), yl_=1 - yl)
    th = ((x + 1) // 2) % 2
    xa = x // 2
    across = (dev(x_=3 - x), y_h)
    next_chip = (lax.rem(tm + 2, 32), mp)
    prev_chip = (lax.rem(tm + 30, 32), mp)

    sent = []

    def remote(src, dst, send_sem, recv_sem, device):
        copy = pltpu.make_async_remote_copy(
            src_ref=src, dst_ref=dst, send_sem=send_sem, recv_sem=recv_sem,
            device_id=device, device_id_type=MESH,
        )
        copy.start()
        sent.append(copy)
        return copy

    loads = []
    for i, (src, dst) in enumerate((
        (q_hbm, qo_ref), (k_hbm, k_ref.at[2]), (v_hbm, v_ref.at[2]),
        (wd_hbm, wd_ref.at[0]),
        *((w.at[:, pl.ds(half * QUART, QUART)], wgu_ref.at[0, :, pl.ds((2 * half + j) * QUART, QUART)])
          for half in range(2) for j, w in enumerate((wg_hbm, wu_hbm))),
    )):
        copy = pltpu.make_async_copy(src, dst, load_sem.at[i])
        copy.start()
        loads.append(copy)

    first = lax.broadcasted_iota(jnp.int32, (8, 128), 0) == 0
    cn_ref[2] = jnp.where(
        first, jnp.full((8, 128), cnt_ref[0], jnp.int32), jnp.full((8, 128), win_ref[0], jnp.int32)
    )

    barrier = pltpu.get_barrier_semaphore()
    partners = (core, y_l, y_h, mate_l, *ups, *x_dev[1:], *xh_dev[1:], next_chip, prev_chip)
    for device in partners:
        pl.semaphore_signal(barrier, inc=1, device_id=device, device_id_type=MESH)
    pl.semaphore_wait(barrier, len(partners))

    kv = (cn_ref, k_ref, v_ref)

    def kv_copy(i, src, dst, sem, device):
        return remote(kv[i].at[src], kv[i].at[dst], kv_send.at[sem, i], kv_recv.at[sem, i], device)

    w_copies = []

    def send_weights(half):
        for j, w in enumerate((wg_hbm, wu_hbm)):
            w_copies.append(remote(
                w.at[:, pl.ds(half * QUART, QUART)], wgu_ref.at[1, :, pl.ds((2 * half + j) * QUART, QUART)],
                w_send.at[2 * half + j], w_recv.at[2 * half + j], mate,
            ))

    below = [kv_copy(0, 2, 0, 0, prev_chip)]
    above = [kv_copy(0, 2, 4, 1, next_chip)]
    loads[0].wait()
    q_copy = remote(qo_ref, q_ref, kv_send.at[4, 0], kv_recv.at[4, 0], prev_chip)
    for i in (1, 2):
        loads[i].wait()
        below.append(kv_copy(i, 2, 0, 0, prev_chip))
        above.append(kv_copy(i, 2, 4, 1, next_chip))
    send_weights(0)

    keys_at = lax.broadcasted_iota(jnp.int32, (1, TOK), 1)
    place = jnp.full((1, TOK), lax.rem(tm + 2, 32), jnp.int32)

    def score(e):
        visible = keys_at < cn_ref[e, 0:1, :]
        if e > 0:
            visible = visible & (cn_ref[0, 1:2, :] >= e) & (place >= e)
        for h in range(WID // HD):
            cols = pl.ds(h * HD, HD)
            s = lax.dot_general(
                q_ref[:, cols], k_ref[e, :, cols], (((1,), (1,)), ((), ())),
                preferred_element_type=jnp.float32,
            ) * HD ** (-0.5)
            s_ref[h, :, pl.ds(e * TOK, TOK)] = jnp.where(visible, s, -1e30)

    q_copy.wait_recv()
    below[0].wait_recv()
    score(2)
    near, mid = [], []
    for i in range(3):
        above[i].wait_recv()
        mid.append(kv_copy(i, 2 * c + 2, 3, 3, core))
    score(4)
    for i in range(3):
        if i > 0:
            below[i].wait_recv()
        near.append(kv_copy(i, 2 * c, 1, 2, core))
    score(0)
    for i in range(3):
        mid[i].wait_recv()
    score(3)
    for i in range(3):
        near[i].wait_recv()
    score(1)

    squares = jnp.zeros((TOK, HD), jnp.float32)
    for h in range(WID // HD):
        cols = pl.ds(h * HD, HD)
        s = s_ref[h]
        expo = jnp.exp(s - jnp.max(s, axis=-1, keepdims=True))
        total = jnp.sum(expo, axis=-1, keepdims=True)
        vals = v_ref[:, :, cols].reshape((WMAX + 1) * TOK, HD)
        att = jnp.dot(expo.astype(jnp.bfloat16), vals, preferred_element_type=jnp.float32) / total
        att_ref[:, cols] = att
        squares = squares + att * att
    row = jnp.broadcast_to(jnp.sum(squares, axis=1, keepdims=True), (TOK, TOK))
    ss_ref[0] = jnp.transpose(row)[0:8]
    ss_copies = [
        remote(ss_ref.at[0], ss_ref.at[j], ss_send.at[j], ss_recv.at[j], device)
        for j, device in enumerate((y_h, *x_dev[1:], *xh_dev[1:]), start=1)
    ]
    for copy in ss_copies:
        copy.wait_recv()
    total = ss_ref[0]
    for j in range(1, 8):
        total = total + ss_ref[j]
    factor = lax.rsqrt(total / D + 1e-06)
    factor = jnp.transpose(jnp.broadcast_to(factor[0:1], (TOK, TOK)))
    for h in range(WID // HD):
        cols = pl.ds(h * HD, HD)
        normed = (att_ref[:, cols] * factor * gain_ref[cols].reshape(1, HD)).astype(jnp.bfloat16)
        nrm_ref[:, :, cols] = normed.reshape(2, HALF, HD)

    y_copies = []

    def spread(i):
        off, size = SPLITS[i]
        rows = pl.ds(off, size)
        x_refs[i][SLOTS[i][0], 0, 0, 0] = nrm_ref[th, rows]
        y_copies.append([
            remote(nrm_ref.at[1 - th, rows], x_refs[i].at[SLOTS[i][0], 0, 1, 0], y_sem.at[0, i, 0], y_sem.at[1, i, 0], mate),
            remote(nrm_ref.at[th, rows], x_refs[i].at[SLOTS[i][0], 0, 0, 1], y_sem.at[0, i, 1], y_sem.at[1, i, 1], y_l),
            remote(nrm_ref.at[1 - th, rows], x_refs[i].at[SLOTS[i][0], 0, 1, 1], y_sem.at[0, i, 2], y_sem.at[1, i, 2], mate_l),
        ])

    ring, relay = {}, {}

    def ring_send(i, way, m):
        sign = (-1, 1)[way]
        src = SLOTS[i][sign * (m - 1)]
        dst = SLOTS[i][4 if m == 4 else sign * m]
        src_ref, dst_ref = x_refs[i].at[src, 0], x_refs[i].at[dst, 0]
        if m == 4:
            src_ref, dst_ref = src_ref.at[way], dst_ref.at[way]
        ring[i, way, m] = remote(
            src_ref, dst_ref, ag_sem.at[0, i, way, m - 1], ag_sem.at[1, i, way, m - 1], ups[way]
        )

    def relay_send(i, slot):
        relay[i, slot] = remote(
            x_refs[i].at[slot, 0], x_refs[i].at[slot, 1], rl_sem.at[0, i, slot], rl_sem.at[1, i, slot], core
        )

    def gather(i, m):
        if m == 0:
            for copy in y_copies[i]:
                copy.wait_recv()
            ring_send(i, 0, 1)
            ring_send(i, 1, 1)
            relay_send(i, SLOTS[i][0])
            return
        for way in range(2):
            ring[i, way, m].wait_recv()
            if m < 4:
                ring_send(i, way, m + 1)
                relay_send(i, SLOTS[i][(-1, 1)[way] * m])
        if m == 4:
            relay_send(i, SLOTS[i][4])

    pa_copies, p_copies, h_copies, hf_copies, o_copies, r_copies, f_copies = {}, {}, {}, {}, {}, {}, {}

    def gate_up(i, m, way):
        slot, count = GROUPS[m]
        size = SPLITS[i][1]
        if way == 0:
            for k in range(slot, slot + count):
                relay[i, k].wait_recv()
        for n in range(way * HID, (way + 1) * HID, 256):
            acc = None
            for half in range(2):
                tokens = x_refs[i][slot : slot + count, :, half].reshape(count * 4 * size, WID)
                part = jnp.dot(tokens, wgu_ref[half, :, n : n + 256], preferred_element_type=jnp.float32)
                acc = part if acc is None else acc + part
            ps_refs[i][slot : slot + count, :, :, :, n : n + 256] = acc.astype(jnp.bfloat16).reshape(
                count, 2, 2, size, 256
            )
        slots = pl.ds(slot, count)
        out = (
            ps_refs[i].at[slots, 1 - xa, :, :, pl.ds(0, HID)],
            ps_refs[i].at[slots, :, 1 - yh, :, pl.ds(HID, HID)],
        )[way]
        pa_copies[i, m, way] = remote(
            out, pa_refs[i].at[slots, way], pa_sem.at[0, i, m, way], pa_sem.at[1, i, m, way], across[way]
        )

    def combine(i, m, way):
        slot, count = GROUPS[m]
        slots = pl.ds(slot, count)
        pa_copies[i, m, way].wait_recv()
        cols = pl.ds(way * HID, HID)
        a, b = ((xa, 1 - yh), (1 - xa, yh))[way]
        for k in range(slot, slot + count):
            ps_refs[i][k, a, b, :, cols] = (
                ps_refs[i][k, a, b, :, cols].astype(jnp.float32)
                + pa_refs[i][k, way, (b, a)[way]].astype(jnp.float32)
            ).astype(jnp.bfloat16)
        p_copies[i, m, way] = remote(
            ps_refs[i].at[slots, a, b, :, cols], pr_refs[i].at[slots, way],
            p_sem.at[0, i, m, way], p_sem.at[1, i, m, way], across[1 - way],
        )

    def hidden(i, m, way):
        slot, count = GROUPS[m]
        slots = pl.ds(slot, count)
        p_copies[i, m, way].wait_recv()
        cols = pl.ds(way * QUART, QUART)
        for k in range(slot, slot + count):
            both = (
                ps_refs[i][k, xa, yh, :, pl.ds(way * HID, HID)].astype(jnp.float32)
                + pa_refs[i][k, way, (yh, xa)[way]].astype(jnp.float32)
                + pr_refs[i][k, way].astype(jnp.float32)
            )
            gate, up = both[:, :QUART], both[:, QUART:]
            h_refs[i][k, xa, yh, :, cols] = (gate / (1.0 + jnp.exp(-gate)) * up).astype(jnp.bfloat16)
        ref = h_refs[i].at[slots, xa, yh, :, cols]
        h_copies[i, m, way] = remote(
            ref, ref, h_sem.at[0, i, m, way], h_sem.at[1, i, m, way], across[1 - way]
        )

    def forward(i, m, way):
        slot, count = GROUPS[m]
        slots = pl.ds(slot, count)
        h_copies[i, m, way].wait_recv()
        cols = pl.ds(way * QUART, QUART)
        ref = (h_refs[i].at[slots, xa, :, :, cols], h_refs[i].at[slots, :, yh, :, cols])[way]
        hf_copies[i, m, way] = remote(
            ref, ref, hf_sem.at[0, i, m, way], hf_sem.at[1, i, m, way], across[way]
        )

    def down(i, m):
        slot, count = GROUPS[m]
        size = SPLITS[i][1]
        for way in range(2):
            hf_copies[i, m, way].wait_recv()
        rows = h_refs[i][slot : slot + count].reshape(count * 4 * size, HID)
        for half in range(2):
            for n in range(0, WID, 256):
                o = jnp.dot(rows, wd_ref[half, :, n : n + 256], preferred_element_type=jnp.float32)
                o = o.reshape(count, 2, 2, size, 256)
                oo_refs[i][slot : slot + count, half, :, :, n : n + 256] = o[:, 0]
                os_refs[i][slot : slot + count, half, :, :, n : n + 256] = o[:, 1].astype(jnp.bfloat16)
        o_copies[i, m] = remote(
            os_refs[i].at[pl.ds(slot, count)], oc_refs[i].at[pl.ds(slot, count)],
            o_sem.at[0, i, m], o_sem.at[1, i, m], core,
        )

    def both_cores(i, m):
        slot, count = GROUPS[m]
        o_copies[i, m].wait_recv()
        for k in range(slot, slot + count):
            oo_refs[i][k] += oc_refs[i][k].astype(jnp.float32)

    def origin(offset):
        return 4 if offset == -3 else offset - 1

    def sums(i, r):
        for way in range(2):
            sign = (1, -1)[way]
            if r == 0:
                rs_refs[i][way, 0, 0] = oo_refs[i][SLOTS[i][3], way].astype(jnp.bfloat16)
                src, dst = rs_refs[i].at[way, 0, 0], rr_refs[i].at[way, 0, way]
            else:
                r_copies[i, way, r - 1].wait_recv()
                slot = SLOTS[i][origin(sign * (4 - r))]
                if r == 1:
                    rs_refs[i][way, 1, way] = (
                        oo_refs[i][slot, way] + rr_refs[i][way, 0, way].astype(jnp.float32)
                    ).astype(jnp.bfloat16)
                    rs_refs[i][way, 1, 1 - way] = oo_refs[i][slot, 1 - way].astype(jnp.bfloat16)
                else:
                    rs_refs[i][way, r] = (
                        oo_refs[i][slot] + rr_refs[i][way, r - 1].astype(jnp.float32)
                    ).astype(jnp.bfloat16)
                src, dst = rs_refs[i].at[way, r], rr_refs[i].at[way, r]
            r_copies[i, way, r] = remote(src, dst, r_sem.at[0, i, way, r], r_sem.at[1, i, way, r], ups[way])

    mine_at = 1 - (z + NZ - 1) // NZ

    def deliver(i):
        for way in range(2):
            r_copies[i, way, 3].wait_recv()
        ref, got, slot = oo_refs[i], rr_refs[i], SLOTS[i][-1]
        ref[slot] += got[0, 3].astype(jnp.float32) + got[1, 3].astype(jnp.float32)
        ref[slot, :, mine_at] += x_refs[i][slot, 0, :, mine_at].astype(jnp.float32)
        for j, (half, group, device) in enumerate(((0, 1 - mine_at, y_l), (1, mine_at, mate), (1, 1 - mine_at, mate_l))):
            f_refs[i][0, j] = ref[slot, half, group].astype(jnp.bfloat16)
            f_copies[i, j] = remote(
                f_refs[i].at[0, j], f_refs[i].at[1, j], f_sem.at[0, i, j], f_sem.at[1, i, j], device
            )

    def finish(i):
        off, size = SPLITS[i]
        rows = pl.ds(off, size)
        for j in range(3):
            f_copies[i, j].wait_recv()
        got = f_refs[i]
        mine = oo_refs[i][SLOTS[i][-1], 0, mine_at] + got[1, 0].astype(jnp.float32)
        theirs = got[1, 1].astype(jnp.float32) + got[1, 2].astype(jnp.float32)
        out_ref[th, rows] = mine.astype(jnp.bfloat16)
        out_ref[1 - th, rows] = theirs.astype(jnp.bfloat16)

    plan = []

    def at(step, order, part, *args):
        plan.append((step, order, len(plan), functools.partial(part, *args)))

    def weights(half):
        for copy in w_copies[2 * half : 2 * half + 2]:
            copy.wait_recv()
        if half == 1:
            w_copies.append(remote(wd_hbm, wd_ref.at[1], w_send.at[4], w_recv.at[4], mate))

    at(SECOND, 0, weights, 1)
    at(DOWN, 9, lambda: w_copies[4].wait_recv())
    done = {}
    for k, (i, m) in enumerate(STEPS):
        for way, begin in enumerate((k, max(k, SECOND))):
            for order, (lag, stage) in enumerate(zip(LAGS, (gate_up, combine, hidden, forward))):
                at(begin + lag, (1, 6, 7, 8)[order], stage, i, m, way)
        begin = max(k, SECOND, DOWN - LAGS[4])
        at(begin + LAGS[4], 10, down, i, m)
        at(begin + LAGS[5], 11, both_cores, i, m)
        done[i, m] = begin + LAGS[5]
    for i, row in enumerate(GATHERS):
        for m, step in enumerate(row):
            if step is not None:
                at(max(step, -1) if step < EARLY else step, 5 if step >= EARLY else -1, gather, i, m)
    for i, hold in enumerate(HOLD):
        step = 0
        for j in range(6):
            part = (sums, sums, sums, sums, deliver, finish)[j]
            step = max(step + 1 + (hold[j] if j > 3 else 0), done[i, max(4 - j, 0)] + (hold[j] if j < 5 else 0))
            if i < 2:
                step = max(step, done[i, 4])
            at(step, 12, part, i, *((j,) if j < 4 else ()))

    for i in range(len(SPLITS)):
        spread(i)
    for copy in w_copies:
        copy.wait_send()
    sent[:] = [copy for copy in sent if all(copy is not old for old in w_copies)]
    send_weights(1)
    gather(0, 0)
    early = [p for p in plan if p[1] == -1]
    for p in sorted(early):
        p[3]()
    for copy in loads[3:]:
        copy.wait()
    weights(0)
    for p in sorted(p for p in plan if p[1] != -1):
        p[3]()

    for copy in sent:
        copy.wait_send()


def per_device(queries, keys, values, window, counts, gain, w_gate, w_up, w_down):
    bf, f32 = jnp.bfloat16, jnp.float32
    n = len(SPLITS)
    sizes = [size for _, size in SPLITS]

    def each(shape_of, dtype):
        return [pltpu.VMEM(shape_of(size), dtype) for size in sizes]

    dma = pltpu.SemaphoreType.DMA
    steps = len(GROUPS)
    scratch = [
        pltpu.VMEM((TOK, WID), bf),
        pltpu.VMEM((TOK, WID), bf),
        pltpu.VMEM((WMAX + 1, TOK, WID), bf),
        pltpu.VMEM((WMAX + 1, TOK, WID), bf),
        pltpu.VMEM((WMAX + 1, 8, 128), jnp.int32),
        pltpu.VMEM((WID // HD, TOK, (WMAX + 1) * TOK), f32),
        pltpu.VMEM((TOK, WID), f32),
        pltpu.VMEM((8, 8, 128), f32),
        pltpu.VMEM((2, HALF, WID), bf),
        pltpu.VMEM((2, WID, 2 * HID), bf),
        pltpu.VMEM((2, HID, WID), bf),
        each(lambda s: (NZ, 2, 2, 2, s, WID), bf),
        each(lambda s: (NZ, 2, 2, s, 2 * HID), bf),
        each(lambda s: (NZ, 2, 2, s, HID), bf),
        each(lambda s: (NZ, 2, s, HID), bf),
        each(lambda s: (NZ, 2, 2, s, HID), bf),
        each(lambda s: (NZ, 2, 2, s, WID), bf),
        each(lambda s: (NZ, 2, 2, s, WID), bf),
        each(lambda s: (NZ, 2, 2, s, WID), f32),
        each(lambda s: (2, 4, 2, 2, s, WID), bf),
        each(lambda s: (2, 4, 2, 2, s, WID), bf),
        each(lambda s: (2, 3, s, WID), bf),
        dma((8,)), dma((5, 3)), dma((5, 3)), dma((5,)), dma((5,)), dma((8,)), dma((8,)),
        dma((2, n, 3)), dma((2, n, 2, 4)), dma((2, n, NZ)), dma((2, n, steps, 2)), dma((2, n, steps, 2)),
        dma((2, n, steps, 2)), dma((2, n, steps, 2)),
        dma((2, n, steps)), dma((2, n, 2, 4)), dma((2, n, 3)),
    ]
    hbm = pl.BlockSpec(memory_space=pl.ANY)
    smem = pl.BlockSpec(memory_space=pltpu.SMEM)
    vmem = pl.BlockSpec(memory_space=pltpu.VMEM)
    out = pl.pallas_call(
        body,
        out_shape=jax.ShapeDtypeStruct((2, HALF, WID), bf),
        in_specs=[hbm, hbm, hbm, smem, smem, vmem, hbm, hbm, hbm],
        out_specs=vmem,
        scratch_shapes=scratch,
        compiler_params=pltpu.CompilerParams(
            collective_id=0, has_side_effects=True, vmem_limit_bytes=60 * 2**20
        ),
        cost_estimate=pl.CostEstimate(flops=10**10, bytes_accessed=3 * 10**6, transcendentals=10**6),
        name="block",
    )(queries, keys, values, window, counts, gain, w_gate, w_up, w_down)
    return out.reshape(TOK, WID)


def solution(mesh):
    in_specs = (
        P("tm", "mp"),
        P("tm", "mp"),
        P("tm", "mp"),
        P("tm"),
        P("tm"),
        P("mp"),
        P("mp", "tm"),
        P("mp", "tm"),
        P("tm", "mp"),
    )
    return jax.shard_map(
        per_device, mesh=mesh, in_specs=in_specs, out_specs=P("tm", "mp"), check_vma=False
    )
```

```python
import functools

import jax
import jax.numpy as jnp
from jax import lax
from jax.experimental import pallas as pl
from jax.experimental.pallas import tpu as pltpu
from jax.sharding import PartitionSpec as P

MESH = pl.DeviceIdType.MESH
HD = 128
D = 6144
WMAX = 4
TOK = 128
HALF = 64
WID = 768
HID = 512
QUART = 256
NX = 4
NZ = 8
SPLITS = ((0, 16), (16, 16), (32, 16), (48, 16))
NEAR = {0: 0, 1: 1, -1: 2, 2: 3, -2: 4, 3: 5, -3: 6, 4: 7}
FAR = {-1: 0, 0: 1, -2: 2, 1: 3, -3: 4, 2: 5, 4: 6, 3: 7}
SLOTS = (NEAR, NEAR, FAR, FAR)
GROUPS = ((0, 1), (1, 2), (3, 2), (5, 2), (7, 1))
STEPS = tuple((i, m) for m in range(5) for i in (0, 1)) + tuple((i, 4 - m) for m in range(5) for i in (2, 3))
LAGS = (0, 1, 2, 3, 4, 5)
GATHERS = ((None, 1, 3, 5, 6), (-13, 2, 4, 6, 7), (-10, 5, 6, 8, 10), (3, 5, 7, 9, 10))
EARLY = 0
SECOND, DOWN = 6, 10
HOLD = ((2, 2, 2, 1, 5, 4), (0, 2, 2, 2, 4, 2), (0, 1, 1, 0, 1, 7), (0, 1, 0, 0, 4, 5))


def body(
    q_hbm, k_hbm, v_hbm, win_ref, cnt_ref, gain_ref, wg_hbm, wu_hbm, wd_hbm, out_ref, *scratch
):
    (qo_ref, q_ref, k_ref, v_ref, cn_ref, s_ref, ss_ref, nrm_ref, wgu_ref, wd_ref) = scratch[:10]
    (x_refs, ps_refs, pa_refs, pr_refs, h_refs, os_refs, oc_refs, oo_refs, rs_refs, rr_refs, f_refs) = scratch[10:21]
    (load_sem, kv_send, kv_recv, w_send, w_recv, ss_sem, out_sem, fac_ref) = scratch[21:29]
    (y_sem, ag_sem, rl_sem, pa_sem, p_sem, h_sem, hf_sem, o_sem, r_sem, f_sem) = scratch[29:39]

    tm = lax.axis_index("tm")
    mp = lax.axis_index("mp")
    yl, z, c = tm // 16, (tm // 2) % NZ, tm % 2
    x, yh = mp // 2, mp % 2

    def dev(yl_=yl, z_=z, c_=c, x_=x, yh_=yh):
        return (yl_ * 16 + z_ * 2 + c_, x_ * 2 + yh_)

    z_up, z_down = lax.rem(z + 1, NZ), lax.rem(z + NZ - 1, NZ)
    core = dev(c_=1 - c)
    y_l, y_h = dev(yl_=1 - yl), dev(yh_=1 - yh)
    ups = (dev(z_=z_up), dev(z_=z_down))
    xs = [lax.rem(x + j, NX) for j in range(NX)]
    x_dev = [dev(x_=xs[j]) for j in range(NX)]
    xh_dev = [dev(x_=xs[j], yh_=1 - yh) for j in range(NX)]
    mate, mate_l = dev(x_=x + 1 - 2 * (x % 2)), dev(x_=x + 1 - 2 * (x % 2), yl_=1 - yl)
    th = ((x + 1) // 2) % 2
    xa = x // 2
    across = (dev(x_=3 - x), y_h)
    yl_dev = [dev(yl_=1 - yl, x_=xs[j], yh_=b) for b in (yh, 1 - yh) for j in range(NX)]
    next_chip = (lax.rem(tm + 2, 32), mp)
    prev_chip = (lax.rem(tm + 30, 32), mp)

    sent = []

    def remote(src, dst, send_sem, recv_sem, device, keep=False):
        copy = pltpu.make_async_remote_copy(
            src_ref=src, dst_ref=dst, send_sem=send_sem, recv_sem=recv_sem,
            device_id=device, device_id_type=MESH,
        )
        copy.start()
        if keep:
            sent.append(copy)
        return copy

    def landed(ref, sem):
        pltpu.make_async_copy(ref, ref, sem).wait()

    loads = []
    for i, (src, dst) in enumerate((
        (q_hbm, qo_ref), (k_hbm, k_ref.at[2]), (v_hbm, v_ref.at[2]),
        (wd_hbm, wd_ref.at[0]),
        *((w.at[:, pl.ds(half * QUART, QUART)], wgu_ref.at[0, :, pl.ds((2 * half + j) * QUART, QUART)])
          for half in range(2) for j, w in enumerate((wg_hbm, wu_hbm))),
    )):
        copy = pltpu.make_async_copy(src, dst, load_sem.at[i])
        copy.start()
        loads.append(copy)

    first = lax.broadcasted_iota(jnp.int32, (8, 128), 0) == 0
    cn_ref[2] = jnp.where(
        first, jnp.full((8, 128), cnt_ref[0], jnp.int32), jnp.full((8, 128), win_ref[0], jnp.int32)
    )

    barrier = pltpu.get_barrier_semaphore()
    partners = (core, y_h, *ups, *x_dev[1:], *xh_dev[1:], next_chip, prev_chip, *yl_dev)
    for device in partners:
        pl.semaphore_signal(barrier, inc=1, device_id=device, device_id_type=MESH)
    pl.semaphore_wait(barrier, len(partners))

    kv = (cn_ref, k_ref, v_ref)

    def kv_copy(i, src, dst, sem, device):
        return remote(kv[i].at[src], kv[i].at[dst], kv_send.at[sem, i], kv_recv.at[sem, i], device, True)

    w_copies = []

    def send_weights(half):
        for j, w in enumerate((wg_hbm, wu_hbm)):
            w_copies.append(remote(
                w.at[:, pl.ds(half * QUART, QUART)], wgu_ref.at[1, :, pl.ds((2 * half + j) * QUART, QUART)],
                w_send.at[2 * half + j], w_recv.at[2 * half + j], mate, True,
            ))

    below = [kv_copy(0, 2, 0, 0, prev_chip)]
    above = [kv_copy(0, 2, 4, 1, next_chip)]
    loads[0].wait()
    q_copy = remote(qo_ref, q_ref, kv_send.at[4, 0], kv_recv.at[4, 0], prev_chip, True)
    for i in (1, 2):
        loads[i].wait()
        below.append(kv_copy(i, 2, 0, 0, prev_chip))
        above.append(kv_copy(i, 2, 4, 1, next_chip))
    send_weights(0)

    keys_at = lax.broadcasted_iota(jnp.int32, (1, TOK), 1)
    place = jnp.full((1, TOK), lax.rem(tm + 2, 32), jnp.int32)

    def score(e):
        visible = keys_at < cn_ref[e, 0:1, :]
        if e > 0:
            visible = visible & (cn_ref[0, 1:2, :] >= e) & (place >= e)
        for h in range(WID // HD):
            cols = pl.ds(h * HD, HD)
            s = lax.dot_general(
                q_ref[:, cols], k_ref[e, :, cols], (((1,), (1,)), ((), ())),
                preferred_element_type=jnp.float32,
            ) * HD ** (-0.5)
            s_ref[h, :, pl.ds(e * TOK, TOK)] = jnp.where(visible, s, -1e30)

    q_copy.wait_recv()
    below[0].wait_recv()
    score(2)
    near, mid = [], []
    for i in range(3):
        above[i].wait_recv()
        mid.append(kv_copy(i, 2 * c + 2, 3, 3, core))
    score(4)
    for i in range(3):
        if i > 0:
            below[i].wait_recv()
        near.append(kv_copy(i, 2 * c, 1, 2, core))
    score(0)
    for i in range(3):
        mid[i].wait_recv()
    score(3)
    for i in range(3):
        near[i].wait_recv()
    score(1)

    squares = jnp.zeros((TOK, HD), jnp.float32)
    for h in range(WID // HD):
        cols = pl.ds(h * HD, HD)
        s = s_ref[h]
        expo = jnp.exp(s - jnp.max(s, axis=-1, keepdims=True))
        total = jnp.sum(expo, axis=-1, keepdims=True)
        vals = v_ref[:, :, cols].reshape((WMAX + 1) * TOK, HD)
        att = jnp.dot(expo.astype(jnp.bfloat16), vals, preferred_element_type=jnp.float32) / total
        nrm_ref[:, :, cols] = (att * gain_ref[cols].reshape(1, HD)).astype(jnp.bfloat16).reshape(2, HALF, HD)
        squares = squares + att * att
    row = jnp.broadcast_to(jnp.sum(squares, axis=1, keepdims=True), (TOK, TOK))
    ss_ref[0] = jnp.transpose(row)[0:8]
    for j, device in enumerate((y_h, *x_dev[1:], *xh_dev[1:], *yl_dev), start=1):
        remote(ss_ref.at[0], ss_ref.at[j], ss_sem.at[0], ss_sem.at[1], device)

    def norm_factors():
        landed(ss_ref.at[pl.ds(1, 15)], ss_sem.at[1])
        for group in range(2):
            total = ss_ref[8 * group]
            for j in range(1, 8):
                total = total + ss_ref[8 * group + j]
            factor = lax.rsqrt(total / D + 1e-06)
            factor = jnp.transpose(jnp.broadcast_to(factor[0:1], (TOK, TOK)))
            fac_ref[group] = factor.reshape(2, HALF, HD)

    y_copies = []

    def spread(i):
        off, size = SPLITS[i]
        rows = pl.ds(off, size)
        x_refs[i][SLOTS[i][0], 0, 0, 0] = nrm_ref[th, rows]
        y_copies.append([
            remote(nrm_ref.at[1 - th, rows], x_refs[i].at[SLOTS[i][0], 0, 1, 0], out_sem.at[0, i], y_sem.at[i], mate),
            remote(nrm_ref.at[th, rows], x_refs[i].at[SLOTS[i][0], 0, 0, 1], out_sem.at[0, i], y_sem.at[i], y_l),
            remote(nrm_ref.at[1 - th, rows], x_refs[i].at[SLOTS[i][0], 0, 1, 1], out_sem.at[0, i], y_sem.at[i], mate_l),
        ])

    ring, relay = {}, {}

    def ring_send(i, way, m):
        sign = (-1, 1)[way]
        src = SLOTS[i][sign * (m - 1)]
        dst = SLOTS[i][4 if m == 4 else sign * m]
        src_ref, dst_ref = x_refs[i].at[src, 0], x_refs[i].at[dst, 0]
        if m == 4:
            src_ref, dst_ref = src_ref.at[way], dst_ref.at[way]
        ring[i, way, m] = remote(
            src_ref, dst_ref, out_sem.at[1, i], ag_sem.at[i, m - 1], ups[way]
        )

    def relay_send(i, slot):
        relay[i, slot] = remote(
            x_refs[i].at[slot, 0], x_refs[i].at[slot, 1], out_sem.at[2, i], rl_sem.at[i, (slot + 1) // 2], core
        )

    def gather(i, m):
        if m == 0:
            landed(f_refs[i].at[1], y_sem.at[i])
            off, size = SPLITS[i]
            at = SLOTS[i][0]
            for group in range(2):
                factor = fac_ref[group, th, pl.ds(off, size)]
                for half in range(2):
                    for h in range(WID // HD):
                        cols = pl.ds(h * HD, HD)
                        x_refs[i][at, 0, half, group, :, cols] = (
                            x_refs[i][at, 0, half, group, :, cols].astype(jnp.float32) * factor
                        ).astype(jnp.bfloat16)
            ring_send(i, 0, 1)
            ring_send(i, 1, 1)
            relay_send(i, SLOTS[i][0])
            return
        if m < 4:
            landed(x_refs[i].at[pl.ds(0, 2), 0], ag_sem.at[i, m - 1])
        else:
            landed(x_refs[i].at[0, 0], ag_sem.at[i, m - 1])
        for way in range(2):
            if m < 4:
                ring_send(i, way, m + 1)
                relay_send(i, SLOTS[i][(-1, 1)[way] * m])
        if m == 4:
            relay_send(i, SLOTS[i][4])

    pa_copies, p_copies, h_copies, hf_copies, o_copies, r_copies, f_copies = {}, {}, {}, {}, {}, {}, {}

    def gate_up(i, m, way):
        slot, count = GROUPS[m]
        size = SPLITS[i][1]
        if way == 0:
            landed(x_refs[i].at[pl.ds(slot, count), 1], rl_sem.at[i, m])
        for n in range(way * HID, (way + 1) * HID, 256):
            acc = None
            for half in range(2):
                tokens = x_refs[i][slot : slot + count, :, half].reshape(count * 4 * size, WID)
                part = jnp.dot(tokens, wgu_ref[half, :, n : n + 256], preferred_element_type=jnp.float32)
                acc = part if acc is None else acc + part
            ps_refs[i][slot : slot + count, :, :, :, n : n + 256] = acc.astype(jnp.bfloat16).reshape(
                count, 2, 2, size, 256
            )
        slots = pl.ds(slot, count)
        out = (
            ps_refs[i].at[slots, 1 - xa, :, :, pl.ds(0, HID)],
            ps_refs[i].at[slots, :, 1 - yh, :, pl.ds(HID, HID)],
        )[way]
        pa_copies[i, m, way] = remote(
            out, pa_refs[i].at[slots, way], out_sem.at[3, i], pa_sem.at[i, m, way], across[way]
        )

    def combine(i, m, way):
        slot, count = GROUPS[m]
        slots = pl.ds(slot, count)
        pa_copies[i, m, way].wait_recv()
        cols = pl.ds(way * HID, HID)
        a, b = ((xa, 1 - yh), (1 - xa, yh))[way]
        for k in range(slot, slot + count):
            ps_refs[i][k, a, b, :, cols] = (
                ps_refs[i][k, a, b, :, cols].astype(jnp.float32)
                + pa_refs[i][k, way, (b, a)[way]].astype(jnp.float32)
            ).astype(jnp.bfloat16)
        p_copies[i, m, way] = remote(
            ps_refs[i].at[slots, a, b, :, cols], pr_refs[i].at[slots, way],
            out_sem.at[4, i], p_sem.at[i, m, way], across[1 - way],
        )

    def hidden(i, m, way):
        slot, count = GROUPS[m]
        slots = pl.ds(slot, count)
        p_copies[i, m, way].wait_recv()
        cols = pl.ds(way * QUART, QUART)
        for k in range(slot, slot + count):
            both = (
                ps_refs[i][k, xa, yh, :, pl.ds(way * HID, HID)].astype(jnp.float32)
                + pa_refs[i][k, way, (yh, xa)[way]].astype(jnp.float32)
                + pr_refs[i][k, way].astype(jnp.float32)
            )
            gate, up = both[:, :QUART], both[:, QUART:]
            h_refs[i][k, xa, yh, :, cols] = (gate / (1.0 + jnp.exp(-gate)) * up).astype(jnp.bfloat16)
        ref = h_refs[i].at[slots, xa, yh, :, cols]
        h_copies[i, m, way] = remote(
            ref, ref, out_sem.at[5, i], h_sem.at[i, m, way], across[1 - way]
        )

    def forward(i, m, way):
        slot, count = GROUPS[m]
        slots = pl.ds(slot, count)
        h_copies[i, m, way].wait_recv()
        cols = pl.ds(way * QUART, QUART)
        ref = (h_refs[i].at[slots, xa, :, :, cols], h_refs[i].at[slots, :, yh, :, cols])[way]
        hf_copies[i, m, way] = remote(
            ref, ref, out_sem.at[6, i], hf_sem.at[i, m], across[way]
        )

    def down(i, m):
        slot, count = GROUPS[m]
        size = SPLITS[i][1]
        landed(h_refs[i].at[pl.ds(slot, count), 0], hf_sem.at[i, m])
        rows = h_refs[i][slot : slot + count].reshape(count * 4 * size, HID)
        for half in range(2):
            for n in range(0, WID, 256):
                o = jnp.dot(rows, wd_ref[half, :, n : n + 256], preferred_element_type=jnp.float32)
                o = o.reshape(count, 2, 2, size, 256)
                oo_refs[i][slot : slot + count, half, :, :, n : n + 256] = o[:, 0]
                os_refs[i][slot : slot + count, half, :, :, n : n + 256] = o[:, 1].astype(jnp.bfloat16)
        o_copies[i, m] = remote(
            os_refs[i].at[pl.ds(slot, count)], oc_refs[i].at[pl.ds(slot, count)],
            out_sem.at[7, i], o_sem.at[i, m], core,
        )

    def both_cores(i, m):
        slot, count = GROUPS[m]
        o_copies[i, m].wait_recv()
        for k in range(slot, slot + count):
            oo_refs[i][k] += oc_refs[i][k].astype(jnp.float32)

    def origin(offset):
        return 4 if offset == -3 else offset - 1

    def sums(i, r):
        if r == 1:
            landed(oc_refs[i].at[0], r_sem.at[i, 0])
        elif r > 1:
            landed(oc_refs[i].at[pl.ds(0, 2)], r_sem.at[i, r - 1])
        for way in range(2):
            sign = (1, -1)[way]
            if r == 0:
                rs_refs[i][way, 0, 0] = oo_refs[i][SLOTS[i][3], way].astype(jnp.bfloat16)
                src, dst = rs_refs[i].at[way, 0, 0], rr_refs[i].at[way, 0, way]
            else:
                slot = SLOTS[i][origin(sign * (4 - r))]
                if r == 1:
                    rs_refs[i][way, 1, way] = (
                        oo_refs[i][slot, way] + rr_refs[i][way, 0, way].astype(jnp.float32)
                    ).astype(jnp.bfloat16)
                    rs_refs[i][way, 1, 1 - way] = oo_refs[i][slot, 1 - way].astype(jnp.bfloat16)
                else:
                    rs_refs[i][way, r] = (
                        oo_refs[i][slot] + rr_refs[i][way, r - 1].astype(jnp.float32)
                    ).astype(jnp.bfloat16)
                src, dst = rs_refs[i].at[way, r], rr_refs[i].at[way, r]
            r_copies[i, way, r] = remote(src, dst, out_sem.at[8, i], r_sem.at[i, r], ups[way])

    mine_at = 1 - (z + NZ - 1) // NZ

    def deliver(i):
        landed(oc_refs[i].at[pl.ds(0, 2)], r_sem.at[i, 3])
        ref, got, slot = oo_refs[i], rr_refs[i], SLOTS[i][-1]
        ref[slot] += got[0, 3].astype(jnp.float32) + got[1, 3].astype(jnp.float32)
        ref[slot, :, mine_at] += x_refs[i][slot, 0, :, mine_at].astype(jnp.float32)
        for j, (half, group, device) in enumerate(((0, 1 - mine_at, y_l), (1, mine_at, mate), (1, 1 - mine_at, mate_l))):
            f_refs[i][0, j] = ref[slot, half, group].astype(jnp.bfloat16)
            f_copies[i, j] = remote(
                f_refs[i].at[0, j], f_refs[i].at[1, j], out_sem.at[9, i], f_sem.at[i], device
            )

    def finish(i):
        off, size = SPLITS[i]
        rows = pl.ds(off, size)
        landed(f_refs[i].at[1], f_sem.at[i])
        got = f_refs[i]
        mine = oo_refs[i][SLOTS[i][-1], 0, mine_at] + got[1, 0].astype(jnp.float32)
        theirs = got[1, 1].astype(jnp.float32) + got[1, 2].astype(jnp.float32)
        out_ref[th, rows] = mine.astype(jnp.bfloat16)
        out_ref[1 - th, rows] = theirs.astype(jnp.bfloat16)

    plan = []

    def at(step, order, part, *args):
        plan.append((step, order, len(plan), functools.partial(part, *args)))

    def weights(half):
        for copy in w_copies[2 * half : 2 * half + 2]:
            copy.wait_recv()
        if half == 1:
            w_copies.append(remote(wd_hbm, wd_ref.at[1], w_send.at[4], w_recv.at[4], mate, True))

    at(SECOND, 0, weights, 1)
    at(DOWN, 9, lambda: w_copies[4].wait_recv())
    done = {}
    for k, (i, m) in enumerate(STEPS):
        for way, begin in enumerate((k, max(k, SECOND))):
            for order, (lag, stage) in enumerate(zip(LAGS, (gate_up, combine, hidden, forward))):
                at(begin + lag, (1, 6, 7, 8)[order], stage, i, m, way)
        begin = max(k, SECOND, DOWN - LAGS[4])
        at(begin + LAGS[4], 10, down, i, m)
        at(begin + LAGS[5], 11, both_cores, i, m)
        done[i, m] = begin + LAGS[5]
    for i, row in enumerate(GATHERS):
        for m, step in enumerate(row):
            if step is not None:
                at(max(step, -1) if step < EARLY else step, 5 if step >= EARLY else -1, gather, i, m)
    for i, hold in enumerate(HOLD):
        step = 0
        for j in range(6):
            part = (sums, sums, sums, sums, deliver, finish)[j]
            step = max(step + 1 + (hold[j] if j > 3 else 0), done[i, max(4 - j, 0)] + (hold[j] if j < 5 else 0))
            if i < 2:
                step = max(step, done[i, 4])
            at(step, 12, part, i, *((j,) if j < 4 else ()))

    for i in range(len(SPLITS)):
        spread(i)
    for copy in w_copies:
        copy.wait_send()
    sent[:] = [copy for copy in sent if all(copy is not old for old in w_copies)]
    send_weights(1)
    norm_factors()
    gather(0, 0)
    early = [p for p in plan if p[1] == -1]
    for p in sorted(early):
        p[3]()
    for copy in loads[3:]:
        copy.wait()
    weights(0)
    for p in sorted(p for p in plan if p[1] != -1):
        p[3]()

    for copy in sent:
        copy.wait_send()
    landed(ss_ref.at[pl.ds(1, 15)], ss_sem.at[0])
    for i in range(len(SPLITS)):
        blocks = oc_refs[i].at[pl.ds(0, 7)]
        for j, ref in enumerate((
            f_refs[i].at[0], blocks, x_refs[i].at[:, 0], pa_refs[i], pr_refs[i], h_refs[i].at[:, 0, 0],
            h_refs[i].at[:, 0], os_refs[i], blocks, f_refs[i].at[0],
        )):
            landed(ref, out_sem.at[j, i])


def per_device(queries, keys, values, window, counts, gain, w_gate, w_up, w_down):
    bf, f32 = jnp.bfloat16, jnp.float32
    n = len(SPLITS)
    sizes = [size for _, size in SPLITS]

    def each(shape_of, dtype):
        return [pltpu.VMEM(shape_of(size), dtype) for size in sizes]

    dma = pltpu.SemaphoreType.DMA
    steps = len(GROUPS)
    scratch = [
        pltpu.VMEM((TOK, WID), bf),
        pltpu.VMEM((TOK, WID), bf),
        pltpu.VMEM((WMAX + 1, TOK, WID), bf),
        pltpu.VMEM((WMAX + 1, TOK, WID), bf),
        pltpu.VMEM((WMAX + 1, 8, 128), jnp.int32),
        pltpu.VMEM((WID // HD, TOK, (WMAX + 1) * TOK), f32),
        pltpu.VMEM((16, 8, 128), f32),
        pltpu.VMEM((2, HALF, WID), bf),
        pltpu.VMEM((2, WID, 2 * HID), bf),
        pltpu.VMEM((2, HID, WID), bf),
        each(lambda s: (NZ, 2, 2, 2, s, WID), bf),
        each(lambda s: (NZ, 2, 2, s, 2 * HID), bf),
        each(lambda s: (NZ, 2, 2, s, HID), bf),
        each(lambda s: (NZ, 2, s, HID), bf),
        each(lambda s: (NZ, 2, 2, s, HID), bf),
        each(lambda s: (NZ, 2, 2, s, WID), bf),
        each(lambda s: (NZ, 2, 2, s, WID), bf),
        each(lambda s: (NZ, 2, 2, s, WID), f32),
        each(lambda s: (2, 4, 2, 2, s, WID), bf),
        each(lambda s: (2, 4, 2, 2, s, WID), bf),
        each(lambda s: (2, 3, s, WID), bf),
        dma((8,)), dma((5, 3)), dma((5, 3)), dma((5,)), dma((5,)), dma((2,)), dma((10, n)),
        pltpu.VMEM((2, 2, HALF, HD), f32),
        dma((n,)), dma((n, 4)), dma((n, steps)), dma((n, steps, 2)), dma((n, steps, 2)), dma((n, steps, 2)),
        dma((n, steps)), dma((n, steps)), dma((n, 4)), dma((n,)),
    ]
    hbm = pl.BlockSpec(memory_space=pl.ANY)
    smem = pl.BlockSpec(memory_space=pltpu.SMEM)
    vmem = pl.BlockSpec(memory_space=pltpu.VMEM)
    out = pl.pallas_call(
        body,
        out_shape=jax.ShapeDtypeStruct((2, HALF, WID), bf),
        in_specs=[hbm, hbm, hbm, smem, smem, vmem, hbm, hbm, hbm],
        out_specs=vmem,
        scratch_shapes=scratch,
        compiler_params=pltpu.CompilerParams(
            collective_id=0, has_side_effects=True, vmem_limit_bytes=60 * 2**20
        ),
        cost_estimate=pl.CostEstimate(flops=10**10, bytes_accessed=3 * 10**6, transcendentals=10**6),
        name="block",
    )(queries, keys, values, window, counts, gain, w_gate, w_up, w_down)
    return out.reshape(TOK, WID)


def solution(mesh):
    in_specs = (
        P("tm", "mp"),
        P("tm", "mp"),
        P("tm", "mp"),
        P("tm"),
        P("tm"),
        P("mp"),
        P("mp", "tm"),
        P("mp", "tm"),
        P("tm", "mp"),
    )
    return jax.shard_map(
        per_device, mesh=mesh, in_specs=in_specs, out_specs=P("tm", "mp"), check_vma=False
    )
```

```python
import functools

import jax
import jax.numpy as jnp
from jax import lax
from jax.experimental import pallas as pl
from jax.experimental.pallas import tpu as pltpu
from jax.sharding import PartitionSpec as P

MESH = pl.DeviceIdType.MESH
HD = 128
D = 6144
WMAX = 4
TOK = 128
HALF = 64
WID = 768
HID = 512
QUART = 256
NX = 4
NZ = 8
SPLITS = ((0, 16), (16, 16), (32, 16), (48, 16))
NEAR = {0: 0, 1: 1, -1: 2, 2: 3, -2: 4, 3: 5, -3: 6, 4: 7}
FAR = {-1: 0, 0: 1, -2: 2, 1: 3, -3: 4, 2: 5, 4: 6, 3: 7}
SLOTS = (NEAR, NEAR, FAR, FAR)
GROUPS = ((0, 1), (1, 2), (3, 2), (5, 2), (7, 1))
STEPS = tuple((i, m) for m in range(5) for i in (0, 1)) + tuple((i, 4 - m) for m in range(5) for i in (2, 3))
LAGS = (0, 1, 2, 3, 4, 5)
GATHERS = ((None, 1, 3, 5, 6), (-13, 2, 4, 6, 7), (-10, 5, 6, 8, 10), (3, 5, 7, 9, 10))
EARLY = 0
SECOND, DOWN = 6, 10
HOLD = ((2, 2, 2, 1, 5, 4), (0, 2, 2, 2, 4, 2), (0, 1, 1, 0, 1, 7), (0, 1, 0, 0, 4, 5))


def body(
    q_hbm, k_hbm, v_hbm, win_ref, cnt_ref, gain_ref, wg_hbm, wu_hbm, wd_hbm, out_ref, *scratch
):
    (qo_ref, q_ref, k_ref, v_ref, cn_ref, s_ref, ss_ref, nrm_ref, wgu_ref, wd_ref) = scratch[:10]
    (x_refs, ps_refs, pa_refs, pr_refs, h_refs, os_refs, oc_refs, oo_refs, rs_refs, rr_refs, f_refs) = scratch[10:21]
    (load_sem, kv_send, kv_recv, w_send, w_recv, ss_sem, out_sem, fac_ref) = scratch[21:29]
    (y_sem, ag_sem, rl_sem, pa_sem, p_sem, h_sem, hf_sem, o_sem, r_sem, f_sem) = scratch[29:39]

    tm = lax.axis_index("tm")
    mp = lax.axis_index("mp")
    yl, z, c = tm // 16, (tm // 2) % NZ, tm % 2
    x, yh = mp // 2, mp % 2

    def dev(yl_=yl, z_=z, c_=c, x_=x, yh_=yh):
        return (yl_ * 16 + z_ * 2 + c_, x_ * 2 + yh_)

    z_up, z_down = lax.rem(z + 1, NZ), lax.rem(z + NZ - 1, NZ)
    core = dev(c_=1 - c)
    y_l, y_h = dev(yl_=1 - yl), dev(yh_=1 - yh)
    ups = (dev(z_=z_up), dev(z_=z_down))
    xs = [lax.rem(x + j, NX) for j in range(NX)]
    x_dev = [dev(x_=xs[j]) for j in range(NX)]
    xh_dev = [dev(x_=xs[j], yh_=1 - yh) for j in range(NX)]
    mate, mate_l = dev(x_=x + 1 - 2 * (x % 2)), dev(x_=x + 1 - 2 * (x % 2), yl_=1 - yl)
    th = ((x + 1) // 2) % 2
    xa = x // 2
    across = (dev(x_=3 - x), y_h)
    yl_dev = [dev(yl_=1 - yl, x_=xs[j], yh_=b) for b in (yh, 1 - yh) for j in range(NX)]
    next_chip = (lax.rem(tm + 2, 32), mp)
    prev_chip = (lax.rem(tm + 30, 32), mp)

    sent = []

    def remote(src, dst, send_sem, recv_sem, device, keep=False):
        copy = pltpu.make_async_remote_copy(
            src_ref=src, dst_ref=dst, send_sem=send_sem, recv_sem=recv_sem,
            device_id=device, device_id_type=MESH,
        )
        copy.start()
        if keep:
            sent.append(copy)
        return copy

    def landed(ref, sem):
        pltpu.make_async_copy(ref, ref, sem).wait()

    loads = []
    for i, (src, dst) in enumerate((
        (q_hbm, qo_ref), (k_hbm, k_ref.at[2]), (v_hbm, v_ref.at[2]),
        (wd_hbm, wd_ref.at[0]),
        *((w.at[:, pl.ds(half * QUART, QUART)], wgu_ref.at[0, :, pl.ds((2 * half + j) * QUART, QUART)])
          for half in range(2) for j, w in enumerate((wg_hbm, wu_hbm))),
    )):
        copy = pltpu.make_async_copy(src, dst, load_sem.at[i])
        copy.start()
        loads.append(copy)

    first = lax.broadcasted_iota(jnp.int32, (8, 128), 0) == 0
    cn_ref[2] = jnp.where(
        first, jnp.full((8, 128), cnt_ref[0], jnp.int32), jnp.full((8, 128), win_ref[0], jnp.int32)
    )

    barrier = pltpu.get_barrier_semaphore()
    partners = (core, y_h, *ups, *x_dev[1:], *xh_dev[1:], next_chip, prev_chip, *yl_dev)
    for device in partners:
        pl.semaphore_signal(barrier, inc=1, device_id=device, device_id_type=MESH)
    pl.semaphore_wait(barrier, len(partners))

    kv = (cn_ref, k_ref, v_ref)

    def kv_copy(i, src, dst, sem, device):
        return remote(kv[i].at[src], kv[i].at[dst], kv_send.at[sem, i], kv_recv.at[sem, i], device, True)

    w_copies = []

    def send_weights(half):
        for j, w in enumerate((wg_hbm, wu_hbm)):
            w_copies.append(remote(
                w.at[:, pl.ds(half * QUART, QUART)], wgu_ref.at[1, :, pl.ds((2 * half + j) * QUART, QUART)],
                w_send.at[2 * half + j], w_recv.at[2 * half + j], mate, True,
            ))

    below = [kv_copy(0, 2, 0, 0, prev_chip)]
    above = [kv_copy(0, 2, 4, 1, next_chip)]
    loads[0].wait()
    q_copy = remote(qo_ref, q_ref, kv_send.at[4, 0], kv_recv.at[4, 0], prev_chip, True)
    for i in (1, 2):
        loads[i].wait()
        if i == 1:
            below.append(kv_copy(i, 2, 0, 0, prev_chip))
        above.append(kv_copy(i, 2, 4, 1, next_chip))
    send_weights(0)

    keys_at = lax.broadcasted_iota(jnp.int32, (1, TOK), 1)
    place = jnp.full((1, TOK), lax.rem(tm + 2, 32), jnp.int32)

    def score(e):
        visible = keys_at < cn_ref[e, 0:1, :]
        if e > 0:
            visible = visible & (cn_ref[0, 1:2, :] >= e) & (place >= e)
        for h in range(WID // HD):
            cols = pl.ds(h * HD, HD)
            s = lax.dot_general(
                q_ref[:, cols], k_ref[e, :, cols], (((1,), (1,)), ((), ())),
                preferred_element_type=jnp.float32,
            ) * HD ** (-0.5)
            s_ref[h, :, pl.ds(e * TOK, TOK)] = jnp.where(visible, s, -1e30)

    q_copy.wait_recv()
    below.append(kv_copy(2, 2, 0, 0, prev_chip))
    below[0].wait_recv()
    near = [kv_copy(0, 2 * c, 1, 2, core)]
    score(2)
    mid = []
    for i in range(3):
        above[i].wait_recv()
        mid.append(kv_copy(i, 2 * c + 2, 3, 3, core))
    score(4)
    below[1].wait_recv()
    near.append(kv_copy(1, 2 * c, 1, 2, core))
    score(0)
    for i in range(3):
        mid[i].wait_recv()
    score(3)
    for i in range(2):
        near[i].wait_recv()
    score(1)
    below[2].wait_recv()
    near.append(kv_copy(2, 2 * c, 1, 2, core))
    near[2].wait_recv()

    squares = jnp.zeros((TOK, HD), jnp.float32)
    for h in range(WID // HD):
        cols = pl.ds(h * HD, HD)
        s = s_ref[h]
        expo = jnp.exp(s - jnp.max(s, axis=-1, keepdims=True))
        total = jnp.sum(expo, axis=-1, keepdims=True)
        vals = v_ref[:, :, cols].reshape((WMAX + 1) * TOK, HD)
        att = jnp.dot(expo.astype(jnp.bfloat16), vals, preferred_element_type=jnp.float32) / total
        nrm_ref[:, :, cols] = (att * gain_ref[cols].reshape(1, HD)).astype(jnp.bfloat16).reshape(2, HALF, HD)
        squares = squares + att * att
    row = jnp.broadcast_to(jnp.sum(squares, axis=1, keepdims=True), (TOK, TOK))
    ss_ref[0] = jnp.transpose(row)[0:8]
    for j, device in enumerate((y_h, *x_dev[1:], *xh_dev[1:], *yl_dev), start=1):
        remote(ss_ref.at[0], ss_ref.at[j], ss_sem.at[0], ss_sem.at[1], device)

    def norm_factors():
        landed(ss_ref.at[pl.ds(1, 15)], ss_sem.at[1])
        for group in range(2):
            total = ss_ref[8 * group]
            for j in range(1, 8):
                total = total + ss_ref[8 * group + j]
            factor = lax.rsqrt(total / D + 1e-06)
            factor = jnp.transpose(jnp.broadcast_to(factor[0:1], (TOK, TOK)))
            fac_ref[group] = factor.reshape(2, HALF, HD)

    y_copies = []

    def spread(i):
        off, size = SPLITS[i]
        rows = pl.ds(off, size)
        x_refs[i][SLOTS[i][0], 0, 0, 0] = nrm_ref[th, rows]
        y_copies.append([
            remote(nrm_ref.at[1 - th, rows], x_refs[i].at[SLOTS[i][0], 0, 1, 0], out_sem.at[0, i], y_sem.at[i], mate),
            remote(nrm_ref.at[th, rows], x_refs[i].at[SLOTS[i][0], 0, 0, 1], out_sem.at[0, i], y_sem.at[i], y_l),
            remote(nrm_ref.at[1 - th, rows], x_refs[i].at[SLOTS[i][0], 0, 1, 1], out_sem.at[0, i], y_sem.at[i], mate_l),
        ])

    ring, relay = {}, {}

    def ring_send(i, way, m):
        sign = (-1, 1)[way]
        src = SLOTS[i][sign * (m - 1)]
        dst = SLOTS[i][4 if m == 4 else sign * m]
        src_ref, dst_ref = x_refs[i].at[src, 0], x_refs[i].at[dst, 0]
        if m == 4:
            src_ref, dst_ref = src_ref.at[way], dst_ref.at[way]
        ring[i, way, m] = remote(
            src_ref, dst_ref, out_sem.at[1, i], ag_sem.at[i, m - 1], ups[way]
        )

    def relay_send(i, slot):
        relay[i, slot] = remote(
            x_refs[i].at[slot, 0], x_refs[i].at[slot, 1], out_sem.at[2, i], rl_sem.at[i, (slot + 1) // 2], core
        )

    def gather(i, m):
        if m == 0:
            landed(f_refs[i].at[1], y_sem.at[i])
            off, size = SPLITS[i]
            at = SLOTS[i][0]
            for group in range(2):
                factor = fac_ref[group, th, pl.ds(off, size)]
                for half in range(2):
                    for h in range(WID // HD):
                        cols = pl.ds(h * HD, HD)
                        x_refs[i][at, 0, half, group, :, cols] = (
                            x_refs[i][at, 0, half, group, :, cols].astype(jnp.float32) * factor
                        ).astype(jnp.bfloat16)
            ring_send(i, 0, 1)
            ring_send(i, 1, 1)
            relay_send(i, SLOTS[i][0])
            return
        if m < 4:
            landed(x_refs[i].at[pl.ds(0, 2), 0], ag_sem.at[i, m - 1])
        else:
            landed(x_refs[i].at[0, 0], ag_sem.at[i, m - 1])
        for way in range(2):
            if m < 4:
                ring_send(i, way, m + 1)
                relay_send(i, SLOTS[i][(-1, 1)[way] * m])
        if m == 4:
            relay_send(i, SLOTS[i][4])

    pa_copies, p_copies, h_copies, hf_copies, o_copies, r_copies, f_copies = {}, {}, {}, {}, {}, {}, {}

    def gate_up(i, m, way):
        slot, count = GROUPS[m]
        size = SPLITS[i][1]
        if way == 0:
            landed(x_refs[i].at[pl.ds(slot, count), 1], rl_sem.at[i, m])
        for n in range(way * HID, (way + 1) * HID, 256):
            acc = None
            for half in range(2):
                tokens = x_refs[i][slot : slot + count, :, half].reshape(count * 4 * size, WID)
                part = jnp.dot(tokens, wgu_ref[half, :, n : n + 256], preferred_element_type=jnp.float32)
                acc = part if acc is None else acc + part
            ps_refs[i][slot : slot + count, :, :, :, n : n + 256] = acc.astype(jnp.bfloat16).reshape(
                count, 2, 2, size, 256
            )
        slots = pl.ds(slot, count)
        out = (
            ps_refs[i].at[slots, 1 - xa, :, :, pl.ds(0, HID)],
            ps_refs[i].at[slots, :, 1 - yh, :, pl.ds(HID, HID)],
        )[way]
        pa_copies[i, m, way] = remote(
            out, pa_refs[i].at[slots, way], out_sem.at[3, i], pa_sem.at[i, m, way], across[way]
        )

    def combine(i, m, way):
        slot, count = GROUPS[m]
        slots = pl.ds(slot, count)
        pa_copies[i, m, way].wait_recv()
        cols = pl.ds(way * HID, HID)
        a, b = ((xa, 1 - yh), (1 - xa, yh))[way]
        for k in range(slot, slot + count):
            ps_refs[i][k, a, b, :, cols] = (
                ps_refs[i][k, a, b, :, cols].astype(jnp.float32)
                + pa_refs[i][k, way, (b, a)[way]].astype(jnp.float32)
            ).astype(jnp.bfloat16)
        p_copies[i, m, way] = remote(
            ps_refs[i].at[slots, a, b, :, cols], pr_refs[i].at[slots, way],
            out_sem.at[4, i], p_sem.at[i, m, way], across[1 - way],
        )

    def hidden(i, m, way):
        slot, count = GROUPS[m]
        slots = pl.ds(slot, count)
        p_copies[i, m, way].wait_recv()
        cols = pl.ds(way * QUART, QUART)
        for k in range(slot, slot + count):
            both = (
                ps_refs[i][k, xa, yh, :, pl.ds(way * HID, HID)].astype(jnp.float32)
                + pa_refs[i][k, way, (yh, xa)[way]].astype(jnp.float32)
                + pr_refs[i][k, way].astype(jnp.float32)
            )
            gate, up = both[:, :QUART], both[:, QUART:]
            h_refs[i][k, xa, yh, :, cols] = (gate / (1.0 + jnp.exp(-gate)) * up).astype(jnp.bfloat16)
        ref = h_refs[i].at[slots, xa, yh, :, cols]
        h_copies[i, m, way] = remote(
            ref, ref, out_sem.at[5, i], h_sem.at[i, m, way], across[1 - way]
        )

    def forward(i, m, way):
        slot, count = GROUPS[m]
        slots = pl.ds(slot, count)
        h_copies[i, m, way].wait_recv()
        cols = pl.ds(way * QUART, QUART)
        ref = (h_refs[i].at[slots, xa, :, :, cols], h_refs[i].at[slots, :, yh, :, cols])[way]
        hf_copies[i, m, way] = remote(
            ref, ref, out_sem.at[6, i], hf_sem.at[i, m], across[way]
        )

    def down(i, m):
        slot, count = GROUPS[m]
        size = SPLITS[i][1]
        landed(h_refs[i].at[pl.ds(slot, count), 0], hf_sem.at[i, m])
        rows = h_refs[i][slot : slot + count].reshape(count * 4 * size, HID)
        for half in range(2):
            for n in range(0, WID, 256):
                o = jnp.dot(rows, wd_ref[half, :, n : n + 256], preferred_element_type=jnp.float32)
                o = o.reshape(count, 2, 2, size, 256)
                oo_refs[i][slot : slot + count, half, :, :, n : n + 256] = o[:, 0]
                os_refs[i][slot : slot + count, half, :, :, n : n + 256] = o[:, 1].astype(jnp.bfloat16)
        o_copies[i, m] = remote(
            os_refs[i].at[pl.ds(slot, count)], oc_refs[i].at[pl.ds(slot, count)],
            out_sem.at[7, i], o_sem.at[i, m], core,
        )

    def both_cores(i, m):
        slot, count = GROUPS[m]
        o_copies[i, m].wait_recv()
        for k in range(slot, slot + count):
            oo_refs[i][k] += oc_refs[i][k].astype(jnp.float32)

    def origin(offset):
        return 4 if offset == -3 else offset - 1

    def sums(i, r):
        if r == 1:
            landed(oc_refs[i].at[0], r_sem.at[i, 0])
        elif r > 1:
            landed(oc_refs[i].at[pl.ds(0, 2)], r_sem.at[i, r - 1])
        for way in range(2):
            sign = (1, -1)[way]
            if r == 0:
                rs_refs[i][way, 0, 0] = oo_refs[i][SLOTS[i][3], way].astype(jnp.bfloat16)
                src, dst = rs_refs[i].at[way, 0, 0], rr_refs[i].at[way, 0, way]
            else:
                slot = SLOTS[i][origin(sign * (4 - r))]
                if r == 1:
                    rs_refs[i][way, 1, way] = (
                        oo_refs[i][slot, way] + rr_refs[i][way, 0, way].astype(jnp.float32)
                    ).astype(jnp.bfloat16)
                    rs_refs[i][way, 1, 1 - way] = oo_refs[i][slot, 1 - way].astype(jnp.bfloat16)
                else:
                    rs_refs[i][way, r] = (
                        oo_refs[i][slot] + rr_refs[i][way, r - 1].astype(jnp.float32)
                    ).astype(jnp.bfloat16)
                src, dst = rs_refs[i].at[way, r], rr_refs[i].at[way, r]
            r_copies[i, way, r] = remote(src, dst, out_sem.at[8, i], r_sem.at[i, r], ups[way])

    mine_at = 1 - (z + NZ - 1) // NZ

    def deliver(i):
        landed(oc_refs[i].at[pl.ds(0, 2)], r_sem.at[i, 3])
        ref, got, slot = oo_refs[i], rr_refs[i], SLOTS[i][-1]
        ref[slot] += got[0, 3].astype(jnp.float32) + got[1, 3].astype(jnp.float32)
        ref[slot, :, mine_at] += x_refs[i][slot, 0, :, mine_at].astype(jnp.float32)
        for j, (half, group, device) in enumerate(((0, 1 - mine_at, y_l), (1, mine_at, mate), (1, 1 - mine_at, mate_l))):
            f_refs[i][0, j] = ref[slot, half, group].astype(jnp.bfloat16)
            f_copies[i, j] = remote(
                f_refs[i].at[0, j], f_refs[i].at[1, j], out_sem.at[9, i], f_sem.at[i], device
            )

    def finish(i):
        off, size = SPLITS[i]
        rows = pl.ds(off, size)
        landed(f_refs[i].at[1], f_sem.at[i])
        got = f_refs[i]
        mine = oo_refs[i][SLOTS[i][-1], 0, mine_at] + got[1, 0].astype(jnp.float32)
        theirs = got[1, 1].astype(jnp.float32) + got[1, 2].astype(jnp.float32)
        out_ref[th, rows] = mine.astype(jnp.bfloat16)
        out_ref[1 - th, rows] = theirs.astype(jnp.bfloat16)

    plan = []

    def at(step, order, part, *args):
        plan.append((step, order, len(plan), functools.partial(part, *args)))

    def weights(half):
        for copy in w_copies[2 * half : 2 * half + 2]:
            copy.wait_recv()
        if half == 1:
            w_copies.append(remote(wd_hbm, wd_ref.at[1], w_send.at[4], w_recv.at[4], mate, True))

    at(SECOND, 0, weights, 1)
    at(DOWN, 9, lambda: w_copies[4].wait_recv())
    done = {}
    for k, (i, m) in enumerate(STEPS):
        for way, begin in enumerate((k, max(k, SECOND))):
            for order, (lag, stage) in enumerate(zip(LAGS, (gate_up, combine, hidden, forward))):
                at(begin + lag, (1, 6, 7, 8)[order], stage, i, m, way)
        begin = max(k, SECOND, DOWN - LAGS[4])
        at(begin + LAGS[4], 10, down, i, m)
        at(begin + LAGS[5], 11, both_cores, i, m)
        done[i, m] = begin + LAGS[5]
    for i, row in enumerate(GATHERS):
        for m, step in enumerate(row):
            if step is not None:
                at(max(step, -1) if step < EARLY else step, 5 if step >= EARLY else -1, gather, i, m)
    for i, hold in enumerate(HOLD):
        step = 0
        for j in range(6):
            part = (sums, sums, sums, sums, deliver, finish)[j]
            step = max(step + 1 + (hold[j] if j > 3 else 0), done[i, max(4 - j, 0)] + (hold[j] if j < 5 else 0))
            if i < 2:
                step = max(step, done[i, 4])
            at(step, 12, part, i, *((j,) if j < 4 else ()))

    for i in range(len(SPLITS)):
        spread(i)
    for copy in w_copies:
        copy.wait_send()
    sent[:] = [copy for copy in sent if all(copy is not old for old in w_copies)]
    send_weights(1)
    norm_factors()
    gather(0, 0)
    early = [p for p in plan if p[1] == -1]
    for p in sorted(early):
        p[3]()
    for copy in loads[3:]:
        copy.wait()
    weights(0)
    for p in sorted(p for p in plan if p[1] != -1):
        p[3]()

    for copy in sent:
        copy.wait_send()
    landed(ss_ref.at[pl.ds(1, 15)], ss_sem.at[0])
    for i in range(len(SPLITS)):
        blocks = oc_refs[i].at[pl.ds(0, 7)]
        for j, ref in enumerate((
            f_refs[i].at[0], blocks, x_refs[i].at[:, 0], pa_refs[i], pr_refs[i], h_refs[i].at[:, 0, 0],
            h_refs[i].at[:, 0], os_refs[i], blocks, f_refs[i].at[0],
        )):
            landed(ref, out_sem.at[j, i])


def per_device(queries, keys, values, window, counts, gain, w_gate, w_up, w_down):
    bf, f32 = jnp.bfloat16, jnp.float32
    n = len(SPLITS)
    sizes = [size for _, size in SPLITS]

    def each(shape_of, dtype):
        return [pltpu.VMEM(shape_of(size), dtype) for size in sizes]

    dma = pltpu.SemaphoreType.DMA
    steps = len(GROUPS)
    scratch = [
        pltpu.VMEM((TOK, WID), bf),
        pltpu.VMEM((TOK, WID), bf),
        pltpu.VMEM((WMAX + 1, TOK, WID), bf),
        pltpu.VMEM((WMAX + 1, TOK, WID), bf),
        pltpu.VMEM((WMAX + 1, 8, 128), jnp.int32),
        pltpu.VMEM((WID // HD, TOK, (WMAX + 1) * TOK), f32),
        pltpu.VMEM((16, 8, 128), f32),
        pltpu.VMEM((2, HALF, WID), bf),
        pltpu.VMEM((2, WID, 2 * HID), bf),
        pltpu.VMEM((2, HID, WID), bf),
        each(lambda s: (NZ, 2, 2, 2, s, WID), bf),
        each(lambda s: (NZ, 2, 2, s, 2 * HID), bf),
        each(lambda s: (NZ, 2, 2, s, HID), bf),
        each(lambda s: (NZ, 2, s, HID), bf),
        each(lambda s: (NZ, 2, 2, s, HID), bf),
        each(lambda s: (NZ, 2, 2, s, WID), bf),
        each(lambda s: (NZ, 2, 2, s, WID), bf),
        each(lambda s: (NZ, 2, 2, s, WID), f32),
        each(lambda s: (2, 4, 2, 2, s, WID), bf),
        each(lambda s: (2, 4, 2, 2, s, WID), bf),
        each(lambda s: (2, 3, s, WID), bf),
        dma((8,)), dma((5, 3)), dma((5, 3)), dma((5,)), dma((5,)), dma((2,)), dma((10, n)),
        pltpu.VMEM((2, 2, HALF, HD), f32),
        dma((n,)), dma((n, 4)), dma((n, steps)), dma((n, steps, 2)), dma((n, steps, 2)), dma((n, steps, 2)),
        dma((n, steps)), dma((n, steps)), dma((n, 4)), dma((n,)),
    ]
    hbm = pl.BlockSpec(memory_space=pl.ANY)
    smem = pl.BlockSpec(memory_space=pltpu.SMEM)
    vmem = pl.BlockSpec(memory_space=pltpu.VMEM)
    out = pl.pallas_call(
        body,
        out_shape=jax.ShapeDtypeStruct((2, HALF, WID), bf),
        in_specs=[hbm, hbm, hbm, smem, smem, vmem, hbm, hbm, hbm],
        out_specs=vmem,
        scratch_shapes=scratch,
        compiler_params=pltpu.CompilerParams(
            collective_id=0, has_side_effects=True, vmem_limit_bytes=60 * 2**20
        ),
        cost_estimate=pl.CostEstimate(flops=10**10, bytes_accessed=3 * 10**6, transcendentals=10**6),
        name="block",
    )(queries, keys, values, window, counts, gain, w_gate, w_up, w_down)
    return out.reshape(TOK, WID)


def solution(mesh):
    in_specs = (
        P("tm", "mp"),
        P("tm", "mp"),
        P("tm", "mp"),
        P("tm"),
        P("tm"),
        P("mp"),
        P("mp", "tm"),
        P("mp", "tm"),
        P("tm", "mp"),
    )
    return jax.shard_map(
        per_device, mesh=mesh, in_specs=in_specs, out_specs=P("tm", "mp"), check_vma=False
    )
```

```python
import functools

import jax
import jax.numpy as jnp
from jax import lax
from jax.experimental import pallas as pl
from jax.experimental.pallas import tpu as pltpu
from jax.sharding import PartitionSpec as P

MESH = pl.DeviceIdType.MESH
HD = 128
D = 6144
WMAX = 4
TOK = 128
HALF = 64
WID = 768
HID = 512
QUART = 256
NX = 4
NZ = 8
SPLITS = ((0, 16), (16, 16), (32, 16), (48, 16))
NEAR = {0: 0, 1: 1, -1: 2, 2: 3, -2: 4, 3: 5, -3: 6, 4: 7}
FAR = {-1: 0, 0: 1, -2: 2, 1: 3, -3: 4, 2: 5, 4: 6, 3: 7}
SLOTS = (NEAR, NEAR, FAR, FAR)
GROUPS = ((0, 1), (1, 2), (3, 2), (5, 2), (7, 1))
STEPS = tuple((i, m) for m in range(5) for i in (0, 1)) + tuple((i, 4 - m) for m in range(5) for i in (2, 3))
LAGS = (0, 1, 2, 3, 4, 5)
GATHERS = ((None, 0, 3, 4, 6), (-2, 2, 4, 6, 7), (-21, 5, 7, 8, 10), (3, 5, 7, 10, 12))
EARLY = -1
SECOND, DOWN = 6, 10
HOLD = ((0, 3, 3, 3, 5, 9), (0, 1, 6, 3, 14, 11), (0, 0, 0, 0, 6, 10), (0, 0, 0, 0, 15, 7))


def body(
    q_hbm, k_hbm, v_hbm, win_ref, cnt_ref, gain_ref, wg_hbm, wu_hbm, wd_hbm, out_ref, *scratch
):
    (qo_ref, q_ref, k_ref, v_ref, cn_ref, s_ref, ss_ref, nrm_ref, wgu_ref, wd_ref) = scratch[:10]
    (x_refs, ps_refs, pa_refs, pr_refs, h_refs, os_refs, oc_refs, oo_refs, rs_refs, rr_refs, f_refs) = scratch[10:21]
    (load_sem, kv_send, kv_recv, w_send, w_recv, ss_sem, out_sem, fac_ref) = scratch[21:29]
    (y_sem, ag_sem, rl_sem, pa_sem, p_sem, h_sem, hf_sem, o_sem, r_sem, f_sem) = scratch[29:39]

    tm = lax.axis_index("tm")
    mp = lax.axis_index("mp")
    yl, z, c = tm // 16, (tm // 2) % NZ, tm % 2
    x, yh = mp // 2, mp % 2

    def dev(yl_=yl, z_=z, c_=c, x_=x, yh_=yh):
        return (yl_ * 16 + z_ * 2 + c_, x_ * 2 + yh_)

    z_up, z_down = lax.rem(z + 1, NZ), lax.rem(z + NZ - 1, NZ)
    core = dev(c_=1 - c)
    y_l, y_h = dev(yl_=1 - yl), dev(yh_=1 - yh)
    ups = (dev(z_=z_up), dev(z_=z_down))
    xs = [lax.rem(x + j, NX) for j in range(NX)]
    x_dev = [dev(x_=xs[j]) for j in range(NX)]
    xh_dev = [dev(x_=xs[j], yh_=1 - yh) for j in range(NX)]
    mate, mate_l = dev(x_=x + 1 - 2 * (x % 2)), dev(x_=x + 1 - 2 * (x % 2), yl_=1 - yl)
    th = ((x + 1) // 2) % 2
    xa = x // 2
    across = (dev(x_=3 - x), y_h)
    yl_dev = [dev(yl_=1 - yl, x_=xs[j], yh_=b) for b in (yh, 1 - yh) for j in range(NX)]
    next_chip = (lax.rem(tm + 2, 32), mp)
    prev_chip = (lax.rem(tm + 30, 32), mp)

    sent = []

    def remote(src, dst, send_sem, recv_sem, device, keep=False):
        copy = pltpu.make_async_remote_copy(
            src_ref=src, dst_ref=dst, send_sem=send_sem, recv_sem=recv_sem,
            device_id=device, device_id_type=MESH,
        )
        copy.start()
        if keep:
            sent.append(copy)
        return copy

    def landed(ref, sem):
        pltpu.make_async_copy(ref, ref, sem).wait()

    loads = []
    for i, (src, dst) in enumerate((
        (q_hbm, qo_ref), (k_hbm, k_ref.at[2]), (v_hbm, v_ref.at[2]),
        (wd_hbm, wd_ref.at[0]),
        *((w.at[:, pl.ds(half * QUART, QUART)], wgu_ref.at[0, :, pl.ds((2 * half + j) * QUART, QUART)])
          for half in range(2) for j, w in enumerate((wg_hbm, wu_hbm))),
    )):
        copy = pltpu.make_async_copy(src, dst, load_sem.at[i])
        copy.start()
        loads.append(copy)

    first = lax.broadcasted_iota(jnp.int32, (8, 128), 0) == 0
    cn_ref[2] = jnp.where(
        first, jnp.full((8, 128), cnt_ref[0], jnp.int32), jnp.full((8, 128), win_ref[0], jnp.int32)
    )

    barrier = pltpu.get_barrier_semaphore()
    partners = (core, y_h, *ups, *x_dev[1:], *xh_dev[1:], next_chip, prev_chip, *yl_dev)
    for device in partners:
        pl.semaphore_signal(barrier, inc=1, device_id=device, device_id_type=MESH)
    pl.semaphore_wait(barrier, len(partners))

    kv = (cn_ref, k_ref, v_ref)

    def kv_copy(i, src, dst, sem, device):
        return remote(kv[i].at[src], kv[i].at[dst], kv_send.at[sem, i], kv_recv.at[sem, i], device, True)

    w_copies = []

    def send_weights(half):
        for j, w in enumerate((wg_hbm, wu_hbm)):
            w_copies.append(remote(
                w.at[:, pl.ds(half * QUART, QUART)], wgu_ref.at[1, :, pl.ds((2 * half + j) * QUART, QUART)],
                w_send.at[2 * half + j], w_recv.at[2 * half + j], mate, True,
            ))

    below = [kv_copy(0, 2, 0, 0, prev_chip)]
    above = [kv_copy(0, 2, 4, 1, next_chip)]
    loads[0].wait()
    q_copy = remote(qo_ref, q_ref, kv_send.at[4, 0], kv_recv.at[4, 0], prev_chip, True)
    for i in (1, 2):
        loads[i].wait()
        below.append(kv_copy(i, 2, 0, 0, prev_chip))
        above.append(kv_copy(i, 2, 4, 1, next_chip))
    send_weights(0)

    keys_at = lax.broadcasted_iota(jnp.int32, (1, TOK), 1)
    place = jnp.full((1, TOK), lax.rem(tm + 2, 32), jnp.int32)

    def score(e):
        visible = keys_at < cn_ref[e, 0:1, :]
        if e > 0:
            visible = visible & (cn_ref[0, 1:2, :] >= e) & (place >= e)
        for h in range(WID // HD):
            cols = pl.ds(h * HD, HD)
            s = lax.dot_general(
                q_ref[:, cols], k_ref[e, :, cols], (((1,), (1,)), ((), ())),
                preferred_element_type=jnp.float32,
            ) * HD ** (-0.5)
            s_ref[h, :, pl.ds(e * TOK, TOK)] = jnp.where(visible, s, -1e30)

    q_copy.wait_recv()
    below[0].wait_recv()
    score(2)
    near, mid = [], []
    for i in range(3):
        above[i].wait_recv()
        mid.append(kv_copy(i, 2 * c + 2, 3, 3, core))
    score(4)
    for i in range(3):
        if i > 0:
            below[i].wait_recv()
        near.append(kv_copy(i, 2 * c, 1, 2, core))
    score(0)
    for i in range(3):
        mid[i].wait_recv()
    score(3)
    for i in range(3):
        near[i].wait_recv()
    score(1)

    squares = jnp.zeros((TOK, HD), jnp.float32)
    for h in range(WID // HD):
        cols = pl.ds(h * HD, HD)
        s = s_ref[h]
        expo = jnp.exp(s - jnp.max(s, axis=-1, keepdims=True))
        total = jnp.sum(expo, axis=-1, keepdims=True)
        vals = v_ref[:, :, cols].reshape((WMAX + 1) * TOK, HD)
        att = jnp.dot(expo.astype(jnp.bfloat16), vals, preferred_element_type=jnp.float32) / total
        nrm_ref[:, :, cols] = (att * gain_ref[cols].reshape(1, HD)).astype(jnp.bfloat16).reshape(2, HALF, HD)
        squares = squares + att * att
    row = jnp.broadcast_to(jnp.sum(squares, axis=1, keepdims=True), (TOK, TOK))
    ss_ref[0] = jnp.transpose(row)[0:8]
    for j, device in enumerate((y_h, *x_dev[1:], *xh_dev[1:], *yl_dev), start=1):
        remote(ss_ref.at[0], ss_ref.at[j], ss_sem.at[0], ss_sem.at[1], device)

    def norm_factors():
        landed(ss_ref.at[pl.ds(1, 15)], ss_sem.at[1])
        for group in range(2):
            total = ss_ref[8 * group]
            for j in range(1, 8):
                total = total + ss_ref[8 * group + j]
            factor = lax.rsqrt(total / D + 1e-06)
            factor = jnp.transpose(jnp.broadcast_to(factor[0:1], (TOK, TOK)))
            fac_ref[group] = factor.reshape(2, HALF, HD)

    y_copies = []

    def spread(i):
        off, size = SPLITS[i]
        rows = pl.ds(off, size)
        x_refs[i][SLOTS[i][0], 0, 0, 0] = nrm_ref[th, rows]
        y_copies.append([
            remote(nrm_ref.at[1 - th, rows], x_refs[i].at[SLOTS[i][0], 0, 1, 0], out_sem.at[0, i], y_sem.at[i], mate),
            remote(nrm_ref.at[th, rows], x_refs[i].at[SLOTS[i][0], 0, 0, 1], out_sem.at[0, i], y_sem.at[i], y_l),
            remote(nrm_ref.at[1 - th, rows], x_refs[i].at[SLOTS[i][0], 0, 1, 1], out_sem.at[0, i], y_sem.at[i], mate_l),
        ])

    ring, relay = {}, {}

    def ring_send(i, way, m):
        sign = (-1, 1)[way]
        src = SLOTS[i][sign * (m - 1)]
        dst = SLOTS[i][4 if m == 4 else sign * m]
        src_ref, dst_ref = x_refs[i].at[src, 0], x_refs[i].at[dst, 0]
        if m == 4:
            src_ref, dst_ref = src_ref.at[way], dst_ref.at[way]
        ring[i, way, m] = remote(
            src_ref, dst_ref, out_sem.at[1, i], ag_sem.at[i, m - 1], ups[way]
        )

    def relay_send(i, slot):
        relay[i, slot] = remote(
            x_refs[i].at[slot, 0], x_refs[i].at[slot, 1], out_sem.at[2, i], rl_sem.at[i, (slot + 1) // 2], core
        )

    def gather(i, m):
        if m == 0:
            landed(f_refs[i].at[1], y_sem.at[i])
            off, size = SPLITS[i]
            at = SLOTS[i][0]
            for group in range(2):
                factor = fac_ref[group, th, pl.ds(off, size)]
                for half in range(2):
                    for h in range(WID // HD):
                        cols = pl.ds(h * HD, HD)
                        x_refs[i][at, 0, half, group, :, cols] = (
                            x_refs[i][at, 0, half, group, :, cols].astype(jnp.float32) * factor
                        ).astype(jnp.bfloat16)
            ring_send(i, 0, 1)
            ring_send(i, 1, 1)
            relay_send(i, SLOTS[i][0])
            return
        if m < 4:
            landed(x_refs[i].at[pl.ds(0, 2), 0], ag_sem.at[i, m - 1])
        else:
            landed(x_refs[i].at[0, 0], ag_sem.at[i, m - 1])
        for way in range(2):
            if m < 4:
                ring_send(i, way, m + 1)
                relay_send(i, SLOTS[i][(-1, 1)[way] * m])
        if m == 4:
            relay_send(i, SLOTS[i][4])

    pa_copies, p_copies, h_copies, hf_copies, o_copies, r_copies, f_copies = {}, {}, {}, {}, {}, {}, {}

    def gate_up(i, m, way):
        slot, count = GROUPS[m]
        size = SPLITS[i][1]
        if way == 0:
            landed(x_refs[i].at[pl.ds(slot, count), 1], rl_sem.at[i, m])
        for n in range(way * HID, (way + 1) * HID, 256):
            acc = None
            for half in range(2):
                tokens = x_refs[i][slot : slot + count, :, half].reshape(count * 4 * size, WID)
                part = jnp.dot(tokens, wgu_ref[half, :, n : n + 256], preferred_element_type=jnp.float32)
                acc = part if acc is None else acc + part
            ps_refs[i][slot : slot + count, :, :, :, n : n + 256] = acc.astype(jnp.bfloat16).reshape(
                count, 2, 2, size, 256
            )
        slots = pl.ds(slot, count)
        out = (
            ps_refs[i].at[slots, 1 - xa, :, :, pl.ds(0, HID)],
            ps_refs[i].at[slots, :, 1 - yh, :, pl.ds(HID, HID)],
        )[way]
        pa_copies[i, m, way] = remote(
            out, pa_refs[i].at[slots, way], out_sem.at[3, i], pa_sem.at[i, m, way], across[way]
        )

    def combine(i, m, way):
        slot, count = GROUPS[m]
        slots = pl.ds(slot, count)
        pa_copies[i, m, way].wait_recv()
        cols = pl.ds(way * HID, HID)
        a, b = ((xa, 1 - yh), (1 - xa, yh))[way]
        for k in range(slot, slot + count):
            ps_refs[i][k, a, b, :, cols] = (
                ps_refs[i][k, a, b, :, cols].astype(jnp.float32)
                + pa_refs[i][k, way, (b, a)[way]].astype(jnp.float32)
            ).astype(jnp.bfloat16)
        p_copies[i, m, way] = remote(
            ps_refs[i].at[slots, a, b, :, cols], pr_refs[i].at[slots, way],
            out_sem.at[4, i], p_sem.at[i, m, way], across[1 - way],
        )

    def hidden(i, m, way):
        slot, count = GROUPS[m]
        slots = pl.ds(slot, count)
        p_copies[i, m, way].wait_recv()
        cols = pl.ds(way * QUART, QUART)
        for k in range(slot, slot + count):
            both = (
                ps_refs[i][k, xa, yh, :, pl.ds(way * HID, HID)].astype(jnp.float32)
                + pa_refs[i][k, way, (yh, xa)[way]].astype(jnp.float32)
                + pr_refs[i][k, way].astype(jnp.float32)
            )
            gate, up = both[:, :QUART], both[:, QUART:]
            h_refs[i][k, xa, yh, :, cols] = (gate / (1.0 + jnp.exp(-gate)) * up).astype(jnp.bfloat16)
        ref = h_refs[i].at[slots, xa, yh, :, cols]
        h_copies[i, m, way] = remote(
            ref, ref, out_sem.at[5, i], h_sem.at[i, m, way], across[1 - way]
        )

    def forward(i, m, way):
        slot, count = GROUPS[m]
        slots = pl.ds(slot, count)
        h_copies[i, m, way].wait_recv()
        cols = pl.ds(way * QUART, QUART)
        ref = (h_refs[i].at[slots, xa, :, :, cols], h_refs[i].at[slots, :, yh, :, cols])[way]
        hf_copies[i, m, way] = remote(
            ref, ref, out_sem.at[6, i], hf_sem.at[i, m], across[way]
        )

    def down(i, m):
        slot, count = GROUPS[m]
        size = SPLITS[i][1]
        landed(h_refs[i].at[pl.ds(slot, count), 0], hf_sem.at[i, m])
        rows = h_refs[i][slot : slot + count].reshape(count * 4 * size, HID)
        for half in range(2):
            for n in range(0, WID, 256):
                o = jnp.dot(rows, wd_ref[half, :, n : n + 256], preferred_element_type=jnp.float32)
                o = o.reshape(count, 2, 2, size, 256)
                oo_refs[i][slot : slot + count, half, :, :, n : n + 256] = o[:, 0]
                os_refs[i][slot : slot + count, half, :, :, n : n + 256] = o[:, 1].astype(jnp.bfloat16)
        o_copies[i, m] = remote(
            os_refs[i].at[pl.ds(slot, count)], oc_refs[i].at[pl.ds(slot, count)],
            out_sem.at[7, i], o_sem.at[i, m], core,
        )

    def both_cores(i, m):
        slot, count = GROUPS[m]
        o_copies[i, m].wait_recv()
        for k in range(slot, slot + count):
            oo_refs[i][k] += oc_refs[i][k].astype(jnp.float32)

    def origin(offset):
        return 4 if offset == -3 else offset - 1

    def sums(i, r):
        if r == 1:
            landed(oc_refs[i].at[0], r_sem.at[i, 0])
        elif r > 1:
            landed(oc_refs[i].at[pl.ds(0, 2)], r_sem.at[i, r - 1])
        for way in range(2):
            sign = (1, -1)[way]
            if r == 0:
                rs_refs[i][way, 0, 0] = oo_refs[i][SLOTS[i][3], way].astype(jnp.bfloat16)
                src, dst = rs_refs[i].at[way, 0, 0], rr_refs[i].at[way, 0, way]
            else:
                slot = SLOTS[i][origin(sign * (4 - r))]
                if r == 1:
                    rs_refs[i][way, 1, way] = (
                        oo_refs[i][slot, way] + rr_refs[i][way, 0, way].astype(jnp.float32)
                    ).astype(jnp.bfloat16)
                    rs_refs[i][way, 1, 1 - way] = oo_refs[i][slot, 1 - way].astype(jnp.bfloat16)
                else:
                    rs_refs[i][way, r] = (
                        oo_refs[i][slot] + rr_refs[i][way, r - 1].astype(jnp.float32)
                    ).astype(jnp.bfloat16)
                src, dst = rs_refs[i].at[way, r], rr_refs[i].at[way, r]
            r_copies[i, way, r] = remote(src, dst, out_sem.at[8, i], r_sem.at[i, r], ups[way])

    mine_at = 1 - (z + NZ - 1) // NZ

    def deliver(i):
        landed(oc_refs[i].at[pl.ds(0, 2)], r_sem.at[i, 3])
        ref, got, slot = oo_refs[i], rr_refs[i], SLOTS[i][-1]
        ref[slot] += got[0, 3].astype(jnp.float32) + got[1, 3].astype(jnp.float32)
        ref[slot, :, mine_at] += x_refs[i][slot, 0, :, mine_at].astype(jnp.float32)
        for j, (half, group, device) in enumerate(((0, 1 - mine_at, y_l), (1, mine_at, mate), (1, 1 - mine_at, mate_l))):
            f_refs[i][0, j] = ref[slot, half, group].astype(jnp.bfloat16)
            f_copies[i, j] = remote(
                f_refs[i].at[0, j], f_refs[i].at[1, j], out_sem.at[9, i], f_sem.at[i], device
            )

    def finish(i):
        off, size = SPLITS[i]
        rows = pl.ds(off, size)
        landed(f_refs[i].at[1], f_sem.at[i])
        got = f_refs[i]
        mine = oo_refs[i][SLOTS[i][-1], 0, mine_at] + got[1, 0].astype(jnp.float32)
        theirs = got[1, 1].astype(jnp.float32) + got[1, 2].astype(jnp.float32)
        out_ref[th, rows] = mine.astype(jnp.bfloat16)
        out_ref[1 - th, rows] = theirs.astype(jnp.bfloat16)

    plan = []

    def at(step, order, part, *args):
        plan.append((step, order, len(plan), functools.partial(part, *args)))

    def weights(half):
        for copy in w_copies[2 * half : 2 * half + 2]:
            copy.wait_recv()
        if half == 1:
            w_copies.append(remote(wd_hbm, wd_ref.at[1], w_send.at[4], w_recv.at[4], mate, True))

    at(SECOND, 0, weights, 1)
    at(DOWN, 9, lambda: w_copies[4].wait_recv())
    done = {}
    for k, (i, m) in enumerate(STEPS):
        for way, begin in enumerate((k, max(k, SECOND))):
            for order, (lag, stage) in enumerate(zip(LAGS, (gate_up, combine, hidden, forward))):
                at(begin + lag, (1, 6, 7, 8)[order], stage, i, m, way)
        begin = max(k, SECOND, DOWN - LAGS[4])
        at(begin + LAGS[4], 10, down, i, m)
        at(begin + LAGS[5], 11, both_cores, i, m)
        done[i, m] = begin + LAGS[5]
    for i, row in enumerate(GATHERS):
        for m, step in enumerate(row):
            if step is not None:
                at(max(step, -1) if step < EARLY else step, 5 if step >= EARLY else -1, gather, i, m)
    for i, hold in enumerate(HOLD):
        step = 0
        for j in range(6):
            part = (sums, sums, sums, sums, deliver, finish)[j]
            step = max(step + 1 + (hold[j] if j > 3 else 0), done[i, max(4 - j, 0)] + (hold[j] if j < 5 else 0))
            if i < 2:
                step = max(step, done[i, 4])
            at(step, 12, part, i, *((j,) if j < 4 else ()))

    for i in range(len(SPLITS)):
        spread(i)
    for copy in w_copies:
        copy.wait_send()
    sent[:] = [copy for copy in sent if all(copy is not old for old in w_copies)]
    send_weights(1)
    norm_factors()
    gather(0, 0)
    early = [p for p in plan if p[1] == -1]
    for p in sorted(early):
        p[3]()
    for copy in loads[3:]:
        copy.wait()
    weights(0)
    for p in sorted(p for p in plan if p[1] != -1):
        p[3]()

    for copy in sent:
        copy.wait_send()
    landed(ss_ref.at[pl.ds(1, 15)], ss_sem.at[0])
    for i in range(len(SPLITS)):
        blocks = oc_refs[i].at[pl.ds(0, 7)]
        for j, ref in enumerate((
            f_refs[i].at[0], blocks, x_refs[i].at[:, 0], pa_refs[i], pr_refs[i], h_refs[i].at[:, 0, 0],
            h_refs[i].at[:, 0], os_refs[i], blocks, f_refs[i].at[0],
        )):
            landed(ref, out_sem.at[j, i])


def per_device(queries, keys, values, window, counts, gain, w_gate, w_up, w_down):
    bf, f32 = jnp.bfloat16, jnp.float32
    n = len(SPLITS)
    sizes = [size for _, size in SPLITS]

    def each(shape_of, dtype):
        return [pltpu.VMEM(shape_of(size), dtype) for size in sizes]

    dma = pltpu.SemaphoreType.DMA
    steps = len(GROUPS)
    scratch = [
        pltpu.VMEM((TOK, WID), bf),
        pltpu.VMEM((TOK, WID), bf),
        pltpu.VMEM((WMAX + 1, TOK, WID), bf),
        pltpu.VMEM((WMAX + 1, TOK, WID), bf),
        pltpu.VMEM((WMAX + 1, 8, 128), jnp.int32),
        pltpu.VMEM((WID // HD, TOK, (WMAX + 1) * TOK), f32),
        pltpu.VMEM((16, 8, 128), f32),
        pltpu.VMEM((2, HALF, WID), bf),
        pltpu.VMEM((2, WID, 2 * HID), bf),
        pltpu.VMEM((2, HID, WID), bf),
        each(lambda s: (NZ, 2, 2, 2, s, WID), bf),
        each(lambda s: (NZ, 2, 2, s, 2 * HID), bf),
        each(lambda s: (NZ, 2, 2, s, HID), bf),
        each(lambda s: (NZ, 2, s, HID), bf),
        each(lambda s: (NZ, 2, 2, s, HID), bf),
        each(lambda s: (NZ, 2, 2, s, WID), bf),
        each(lambda s: (NZ, 2, 2, s, WID), bf),
        each(lambda s: (NZ, 2, 2, s, WID), f32),
        each(lambda s: (2, 4, 2, 2, s, WID), bf),
        each(lambda s: (2, 4, 2, 2, s, WID), bf),
        each(lambda s: (2, 3, s, WID), bf),
        dma((8,)), dma((5, 3)), dma((5, 3)), dma((5,)), dma((5,)), dma((2,)), dma((10, n)),
        pltpu.VMEM((2, 2, HALF, HD), f32),
        dma((n,)), dma((n, 4)), dma((n, steps)), dma((n, steps, 2)), dma((n, steps, 2)), dma((n, steps, 2)),
        dma((n, steps)), dma((n, steps)), dma((n, 4)), dma((n,)),
    ]
    hbm = pl.BlockSpec(memory_space=pl.ANY)
    smem = pl.BlockSpec(memory_space=pltpu.SMEM)
    vmem = pl.BlockSpec(memory_space=pltpu.VMEM)
    out = pl.pallas_call(
        body,
        out_shape=jax.ShapeDtypeStruct((2, HALF, WID), bf),
        in_specs=[hbm, hbm, hbm, smem, smem, vmem, hbm, hbm, hbm],
        out_specs=vmem,
        scratch_shapes=scratch,
        compiler_params=pltpu.CompilerParams(
            collective_id=0, has_side_effects=True, vmem_limit_bytes=60 * 2**20
        ),
        cost_estimate=pl.CostEstimate(flops=10**10, bytes_accessed=3 * 10**6, transcendentals=10**6),
        name="block",
    )(queries, keys, values, window, counts, gain, w_gate, w_up, w_down)
    return out.reshape(TOK, WID)


def solution(mesh):
    in_specs = (
        P("tm", "mp"),
        P("tm", "mp"),
        P("tm", "mp"),
        P("tm"),
        P("tm"),
        P("mp"),
        P("mp", "tm"),
        P("mp", "tm"),
        P("tm", "mp"),
    )
    return jax.shard_map(
        per_device, mesh=mesh, in_specs=in_specs, out_specs=P("tm", "mp"), check_vma=False
    )
```
